32 devices in a mesh: dp: 4 (over y, core), table: 8 (over z, x).
Axes of the slice: x: 2, y: 2, z: 4, core: 2. Of those that a mesh axis runs over, the one named last changes fastest.
Arguments:
- embedded: bfloat16 [2, 2048, 4096], P(None, 'dp', 'table'), may hold values from -1.1953125 to 1.1953125
- resid_grad: bfloat16 [2, 2048, 4096], P(None, 'dp', 'table'), may hold values from -0.29882812 to 0.29882812
- query_grad: bfloat16 [2, 2048, 2048], P(None, ('dp', 'table')), may hold values from -0.59765625 to 0.59765625
- query_weight: bfloat16 [4096, 2048], P('table'), may hold values from -0.09375 to 0.09375
- ngram_rows: int32 [2, 2048, 4], P(None, 'dp'), may hold values from 0 to 799999, as said below
- touched_rows: int32 [8, 4, 12], replicated, may hold values from -1 to 799999, as said below
- row_values: float32 [8, 4, 12, 1024], P('table'), may hold values from -6 to 6
- row_mean: float32 [8, 4, 12, 1024], P('table'), may hold values from -0.6 to 0.6
- row_square: float32 [8, 4, 12, 1024], P('table'), may hold values from 0.01 to 0.1
Outputs:
- weight_grad: float32 [4096, 2048], P('table')
- new_values: float32 [8, 4, 12, 1024], P('table')
- new_mean: float32 [8, 4, 12, 1024], P('table')
- new_square: float32 [8, 4, 12, 1024], P('table')
The draws below stay inside these ranges and needn't reach their ends.
Inputs may be any that keep to these rules, and one draw needn't show every extreme that they name: `touched_rows`: owner o's list for slice s holds 1 to 12 distinct row ids of [o * 100000, (o + 1) * 100000) first, then -1; in every slice some owner's list is full. `ngram_rows`: every id of slice s is one of the listed rows of owner id // 100000 for slice s.
All inputs are finite; a program needn't handle non-finite values.
Results may differ from the reference program's by a relative error of at most 0.0003.
Values may be sent and summed in bfloat16 or wider, within the bound.
A program may use at most 64 MiB of HBM per device.

```python
import math
import jax
import jax.numpy as jnp

SLICES = 4
SW = 1024
D = 4096
HQ = 2048
MICRO = 2
US = 12
SHARD_ROWS = 100000
TOKENS = 2048
N_TABLE = 8


def listed_rows(key):
    base = jax.random.fold_in(key, 7)
    key_count, key_full, key_offset = jax.random.split(base, 3)
    counts = jax.random.randint(key_count, (N_TABLE, SLICES), 1, US + 1)
    fullest = jax.random.randint(key_full, (SLICES,), 0, N_TABLE)
    owners = jnp.arange(N_TABLE, dtype=jnp.int32)
    counts = jnp.where(owners[:, None] == fullest[None, :], US, counts).astype(jnp.int32)
    stride = SHARD_ROWS // US
    offsets = jax.random.randint(key_offset, (N_TABLE, SLICES, US), 0, stride)
    entries = jnp.arange(US, dtype=jnp.int32)
    rows = owners[:, None, None] * SHARD_ROWS + entries[None, None, :] * stride + offsets
    live = entries[None, None, :] < counts[:, :, None]
    return (jnp.where(live, rows, -1).astype(jnp.int32), counts)


def draw_touched_rows(key, part):
    return listed_rows(key)[0]


def draw_ngram_rows(key, part):
    lists, counts = listed_rows(key)
    starts = jnp.cumsum(counts, axis=0) - counts
    totals = jnp.sum(counts, axis=0)
    picks = jax.random.randint(jax.random.fold_in(key, 11), (MICRO, TOKENS, SLICES), 0, totals[None, None, :])
    starts_t = starts.T
    owner = jnp.sum((picks[..., None] >= starts_t[None, None, :, :]).astype(jnp.int32), axis=-1) - 1
    chosen = jnp.arange(N_TABLE, dtype=jnp.int32)[None, None, None, :] == owner[..., None]
    first = jnp.sum(jnp.where(chosen, starts_t[None, None, :, :], 0), axis=-1)
    entry = picks - first
    slot_ids = jnp.arange(SLICES, dtype=jnp.int32)[None, None, :]
    return lists[owner, slot_ids, entry].astype(jnp.int32)


def shard_levels(rng, dims, cuts, least, top_value):
    factor_of, own = 1.0, jax.random.fold_in(rng, 6)
    for dim, blocks in cuts:
        heights = jnp.exp(jax.random.uniform(jax.random.fold_in(own, dim), (blocks,), jnp.float32, least / len(cuts), top_value / len(cuts)))
        factor_of = factor_of * jnp.repeat(heights, dims[dim] // blocks).reshape([-1 if axis == dim else 1 for axis in range(len(dims))])
    return factor_of


def bell_draw(key, shape, spread, limit, shards=(), held_as=jnp.bfloat16):
    factor_of = shard_levels(key, shape, shards, -0.22, 0.18) if shards else 1.0
    drawn = jax.random.normal(key, shape, jnp.float32) * spread * factor_of
    return jnp.minimum(jnp.maximum(drawn, -limit), limit).astype(held_as)


def setup_inputs(seed: int = 0) -> dict:
    splits = jax.random.split(jax.random.key(seed), 10)
    return {
        "embedded": bell_draw(splits[0], (MICRO, TOKENS, D), 0.2, 1.1953125, ((1, 4), (2, 8))),
        "resid_grad": bell_draw(splits[1], (MICRO, TOKENS, D), 0.05, 0.29882812, ((1, 4), (2, 8))),
        "query_grad": bell_draw(splits[2], (MICRO, TOKENS, HQ), 0.1, 0.59765625, ((1, 32),)),
        "query_weight": bell_draw(splits[3], (D, HQ), D ** -0.5, 0.09375, ((0, 8),)),
        "ngram_rows": draw_ngram_rows(jax.random.fold_in(splits[9], 71), 0),
        "touched_rows": draw_touched_rows(jax.random.fold_in(splits[9], 71), 0),
        "row_values": bell_draw(splits[6], (N_TABLE, SLICES, US, SW), 1.0, 6.0, ((0, 8),), jnp.float32),
        "row_mean": bell_draw(splits[7], (N_TABLE, SLICES, US, SW), 0.1, 0.6, ((0, 8),), jnp.float32),
        "row_square": jnp.clip(jnp.exp(math.log(0.1) - 2.3025851 * jax.random.uniform(splits[8], (N_TABLE, SLICES, US, SW), jnp.float32) ** shard_levels(splits[8], (N_TABLE, SLICES, US, SW), ((0, 8),), -0.2, 0.2)), 0.01, 0.1),
    }


beta_one = 0.9
beta_two = 0.95
learn_rate = 0.01
adam_eps = 1e-08
adam_step = 10

def adam_rows(grads, values, mean, square, live):
    corr_one = 1.0 - beta_one ** adam_step
    corr_two = 1.0 - beta_two ** adam_step
    mean_next = beta_one * mean + (1.0 - beta_one) * grads
    square_next = beta_two * square + (1.0 - beta_two) * grads * grads
    update = learn_rate * (mean_next / corr_one) / (jnp.sqrt(square_next / corr_two) + adam_eps)
    values_next = values - update
    return (jnp.where(live, values_next, values), jnp.where(live, mean_next, mean), jnp.where(live, square_next, square))

def reference(embedded, resid_grad, query_grad, query_weight, ngram_rows, touched_rows, row_values, row_mean, row_square):
    wgrad = jnp.zeros((D, HQ), jnp.float32)
    seg_total = jnp.zeros((SLICES, N_TABLE * US, SW), jnp.float32)
    for micro in range(MICRO):
        back = jnp.dot(query_grad[micro], query_weight.T, preferred_element_type=jnp.float32)
        emb_grad = resid_grad[micro].astype(jnp.float32) + back
        wgrad = wgrad + jnp.dot(embedded[micro].T, query_grad[micro], preferred_element_type=jnp.float32)
        for slot in range(SLICES):
            ids = ngram_rows[micro, :, slot]
            owner = (ids // SHARD_ROWS).astype(jnp.int32)
            listed = touched_rows[owner, slot, :]
            where_hit = jnp.argmax((listed == ids[:, None]).astype(jnp.int32), axis=1).astype(jnp.int32)
            segment = owner * US + where_hit
            piece = emb_grad[:, slot * SW:(slot + 1) * SW]
            summed = jax.ops.segment_sum(piece, segment, num_segments=N_TABLE * US)
            seg_total = seg_total.at[slot].add(summed)
    grads = seg_total.reshape(SLICES, N_TABLE, US, SW).transpose(1, 0, 2, 3)
    live = (touched_rows >= 0)[..., None]
    values_next, mean_next, square_next = adam_rows(grads, row_values, row_mean, row_square, live)
    return (wgrad, values_next, mean_next, square_next)
```

```python
import functools

import jax
import jax.numpy as jnp
from jax import lax
from jax.experimental import pallas as pl
from jax.experimental.pallas import tpu as pltpu
from jax.sharding import PartitionSpec as P

SLICES = 4
SW = 1024


beta_one = 0.9
beta_two = 0.95
learn_rate = 0.01
adam_eps = 1e-08
adam_step = 10


def adam_rows(grads, values, mean, square, live):
    corr_one = 1.0 - beta_one**adam_step
    corr_two = 1.0 - beta_two**adam_step
    mean_next = beta_one * mean + (1.0 - beta_one) * grads
    square_next = beta_two * square + (1.0 - beta_two) * grads * grads
    update = learn_rate * (mean_next / corr_one) / (jnp.sqrt(square_next / corr_two) + adam_eps)
    values_next = values - update
    return (
        jnp.where(live, values_next, values),
        jnp.where(live, mean_next, mean),
        jnp.where(live, square_next, square),
    )


def make_step(emb_part, weight_part, carry, piece):
    back_part, wgrad = carry
    back = jnp.einsum("mrh,ph->mrp", piece, weight_part, preferred_element_type=jnp.float32)
    back_part = back
    wgrad = wgrad + jnp.einsum("mrp,mrh->ph", emb_part, piece, preferred_element_type=jnp.float32)
    return (back_part, wgrad)


def local(
    embedded,
    resid_grad,
    query_grad,
    query_weight,
    ngram_rows,
    touched_rows,
    row_values,
    row_mean,
    row_square,
):
    micro_count, group_tokens, width_part = embedded.shape
    hidden = query_grad.shape[2]
    tables = lax.axis_size("table")
    table_idx = lax.axis_index("table")
    zero_grad = jnp.zeros((width_part, hidden), jnp.float32)
    wgrad = zero_grad
    backs = []
    for micro in range(micro_count):
        start_back = jnp.zeros((1, group_tokens, width_part), jnp.float32)
        back_one, wgrad = make_step(
            embedded[micro : micro + 1],
            query_weight,
            (start_back, wgrad),
            lax.all_gather(query_grad[micro : micro + 1], "table", axis=1, tiled=True),
        )
        backs.append(back_one)
    back_all = jnp.concatenate(backs, axis=0)
    emb_grad = resid_grad.astype(jnp.float32) + back_all
    weight_grad = lax.psum(wgrad, "dp")
    slice_idx = table_idx * width_part // SW
    ids = lax.dynamic_index_in_dim(ngram_rows, slice_idx, 2, False)
    listed = lax.dynamic_index_in_dim(touched_rows, slice_idx, 1, False)
    entries = listed.shape[1]
    flat_list = listed.reshape(tables * entries)
    onehot = (ids[:, :, None] == flat_list[None, None, :]).astype(jnp.float32)
    buckets = jnp.einsum(
        "mtk,mtp->kp",
        onehot,
        emb_grad,
        precision=lax.Precision.HIGHEST,
        preferred_element_type=jnp.float32,
    )
    buckets = buckets.reshape(tables, entries, width_part)
    arrived = lax.all_to_all(buckets, "table", split_axis=0, concat_axis=0, tiled=True)
    per_slice = tables // SLICES
    local_grad = (
        arrived.reshape(SLICES, per_slice, entries, width_part)
        .transpose(0, 2, 1, 3)
        .reshape(SLICES, entries, per_slice * width_part)
    )
    mine = lax.dynamic_index_in_dim(touched_rows, table_idx, 0, False)
    live = (mine >= 0)[..., None]
    values = row_values[0]
    mean = row_mean[0]
    square = row_square[0]
    grads = lax.psum(local_grad, "dp")
    values_next, mean_next, square_next = adam_rows(grads, values, mean, square, live)
    return (weight_grad, values_next[None], mean_next[None], square_next[None])


CHUNKS = 8
SLOT = 16
MESH = pl.DeviceIdType.MESH
UP, DOWN, ACROSS = 0, 1, 2


def kernel(
    emb_hbm,
    resid_hbm,
    qg_hbm,
    w_hbm,
    onehot,
    out_hbm,
    grads_out,
    emb,
    emb_t,
    resid,
    w,
    gq,
    part_own,
    part_send,
    part_recv,
    q_send,
    q_recv,
    s_send,
    s_recv,
    res,
    bucket,
    b_send,
    b_recv,
    y_send,
    y_recv,
    a_send,
    a_recv,
    sib_recv,
    load_sem,
    g_send_sem,
    g_recv_sem,
    p_sem,
    q_sem,
    s_sem,
    f_sem,
    o_sem,
    b_sem,
    y_sem,
    a_send_sem,
    a_recv_sem,
    h_sem,
):
    dp, me = lax.axis_index("dp"), lax.axis_index("table")
    y, core = dp // 2, dp % 2
    z, x = me // 2, me % 2
    sib = dp + 1 - 2 * core
    ynb = (1 - y) * 2 + core
    zpair = z + 1 - 2 * (z % 2)
    micro, mine, hidden = qg_hbm.shape
    cols = hidden // CHUNKS
    rows = emb_t.shape[0] // 2

    barrier = pltpu.get_barrier_semaphore()
    for step in range(1, 8):
        pl.semaphore_signal(barrier, inc=1, device_id=(dp, (me + step) % 8), device_id_type=MESH)
    pl.semaphore_signal(barrier, inc=1, device_id=(sib, me), device_id_type=MESH)
    pl.semaphore_signal(barrier, inc=1, device_id=(ynb, me), device_id_type=MESH)

    loads = [
        pltpu.make_async_copy(emb_hbm, emb, load_sem.at[0]),
        pltpu.make_async_copy(resid_hbm, resid, load_sem.at[1]),
        pltpu.make_async_copy(w_hbm, w, load_sem.at[2]),
    ]
    for load in loads:
        load.start()

    def span(c):
        return pl.ds(pl.multiple_of(c * cols, cols), cols)

    def tokens(t):
        return pl.ds(pl.multiple_of(t * mine, mine), mine)

    def held(c, t):
        return gq.at[c, :, tokens(t), :]

    def own_load(c):
        return pltpu.make_async_copy(qg_hbm.at[:, :, span(c)], held(c, me), load_sem.at[3 + c])

    for c in range(CHUNKS):
        own_load(c).start()

    pl.semaphore_wait(barrier, 9)

    def shard_copy(c, t, way, source=None):
        to_z = z + 1 if way == UP else z - 1
        to = (dp, to_z * 2 + x) if way != ACROSS else (dp, z * 2 + 1 - x)
        return pltpu.make_async_remote_copy(
            src_ref=held(c, t) if source is None else source,
            dst_ref=held(c, t),
            send_sem=g_send_sem.at[c, t, way],
            recv_sem=g_recv_sem.at[c, t],
            device_id=to,
            device_id_type=MESH,
        )

    def arrived(c, t):
        shard_copy(c, t, ACROSS).wait_recv()

    def each_own(c, act):
        own = qg_hbm.at[:, :, span(c)]

        @pl.when(z < 3)
        def _():
            act(shard_copy(c, me, UP, own))

        @pl.when(z > 0)
        def _():
            act(shard_copy(c, me, DOWN, own))

        act(shard_copy(c, me, ACROSS, own))

    def each_forward(c, far, act, wait):
        for sign, way in ((-1, UP), (1, DOWN)):
            from_z = z + sign * far
            t = from_z * 2 + x
            there = from_z >= 0 if sign < 0 else from_z < 4
            onward = z < 3 if way == UP else z > 0

            @pl.when(there)
            def _():
                if wait:
                    arrived(c, t)

                @pl.when(onward)
                def _():
                    act(shard_copy(c, t, way))

                if far == 1:

                    @pl.when((c % 2 == 0) | (from_z != zpair))
                    def _():
                        act(shard_copy(c, t, ACROSS))
                else:
                    act(shard_copy(c, t, ACROSS))

    def each_relay(c, act, wait):
        t = z * 2 + 1 - x

        @pl.when(c % 2 == 1)
        def _():
            if wait:
                arrived(c, t)

            @pl.when(z % 2 == 0)
            def _():
                act(shard_copy(c, t, UP))

            @pl.when(z % 2 == 1)
            def _():
                act(shard_copy(c, t, DOWN))

    def start(copy):
        copy.start()

    def sibling_copy(src, dst, sems):
        return pltpu.make_async_remote_copy(
            src_ref=src, dst_ref=dst, send_sem=sems.at[0], recv_sem=sems.at[1], device_id=(sib, me), device_id_type=MESH
        )

    def y_copy(src, dst, sems):
        return pltpu.make_async_remote_copy(
            src_ref=src, dst_ref=dst, send_sem=sems.at[0], recv_sem=sems.at[1], device_id=(ynb, me), device_id_type=MESH
        )

    def part_copy(c):
        return sibling_copy(part_send.at[c], part_recv.at[c], p_sem.at[c])

    def q_copy(c):
        return y_copy(q_send.at[c], q_recv.at[c], q_sem.at[c])

    def s_copy(c):
        return y_copy(s_send.at[c], s_recv.at[c], s_sem.at[c])

    def out_rows(k):
        return pl.ds(pl.multiple_of(k * rows, rows), rows)

    def final_copy(c):
        return sibling_copy(res.at[c], out_hbm.at[out_rows(core), span(c)], f_sem.at[c])

    def out_copy(c):
        return pltpu.make_async_copy(res.at[c], out_hbm.at[out_rows(core), span(c)], o_sem.at[c])

    def dot(a, b):
        return jnp.dot(a, b, preferred_element_type=jnp.float32)

    def dot_nt(a, b):
        return lax.dot_general(a, b, (((1,), (1,)), ((), ())), preferred_element_type=jnp.float32)

    def compute(c):
        for far in (1, 2, 3):
            other = (z + far) % 4
            arrived(c, other * 2 + 1 - x)

        @pl.when(c % 2 == 0)
        def _():
            arrived(c, z * 2 + 1 - x)

        own_load(c).wait()
        block = gq[c].reshape(micro * mine * 8, cols)
        part_send[c] = dot(emb_t[out_rows(1 - core), :], block)
        part_copy(c).start()
        part_own[c] = dot(emb_t[out_rows(core), :], block)
        sums = dot(onehot[...], block)
        high = sums.astype(jnp.bfloat16)
        rest = sums - high.astype(jnp.float32)
        mid = rest.astype(jnp.bfloat16)
        low = (rest - mid.astype(jnp.float32)).astype(jnp.bfloat16)
        w_part = w[:, span(c)]
        bucket[...] += dot_nt(high, w_part) + dot_nt(mid, w_part) + dot_nt(low, w_part)

    def core_sum(c):
        part_copy(c).wait_recv()
        total = part_own[c] + part_recv[c]
        top = jnp.maximum(jnp.max(jnp.abs(total), axis=0, keepdims=True), 1e-30)
        codes = jnp.round(total * (32767.0 / top))
        q_send[c] = codes.astype(jnp.int32).astype(jnp.int16)
        s_send[c] = jnp.broadcast_to(top * (1.0 / 32767.0), s_send.shape[1:])
        q_copy(c).start()
        s_copy(c).start()

    def finish(c):
        q_copy(c).wait_recv()
        s_copy(c).wait_recv()
        here = q_send[c].astype(jnp.int32).astype(jnp.float32) * s_send[c][0:1, :]
        there = q_recv[c].astype(jnp.int32).astype(jnp.float32) * s_recv[c][0:1, :]
        res[c] = jnp.where(y == 0, here, there) + jnp.where(y == 0, there, here)
        final_copy(c).start()
        out_copy(c).start()

    def guarded(c, stage):
        @pl.when((c >= 0) & (c < CHUNKS))
        def _():
            stage(c)

    def forward_stage(far):
        def stage(c):
            each_forward(c, far, start, True)
            if far == 1:
                each_relay(c, start, True)

        return stage

    for c in range(2):
        each_own(c, start)

    loads[0].wait()
    group = mine * 8
    for m in range(micro):
        emb_t[:, m * group : (m + 1) * group] = emb[m].T
    loads[1].wait()
    bucket[...] = dot(onehot[:, 0:group], resid[0]) + dot(onehot[:, group : 2 * group], resid[1])
    loads[2].wait()

    def slot(s, carry):
        guarded(s, lambda c: each_own(c, start))
        guarded(s - 2, forward_stage(1))
        guarded(s - 3, forward_stage(2))
        guarded(s - 4, forward_stage(3))
        guarded(s - 5, compute)
        guarded(s - 6, core_sum)
        guarded(s - 8, finish)
        return carry

    lax.fori_loop(2, CHUNKS + 5, slot, 0)

    half = b_send.shape[1]

    def half_cols(k):
        return pl.ds(pl.multiple_of(k * half, half), half)

    b_copy = sibling_copy(b_send, b_recv, b_sem)
    b_send[...] = bucket[:, half_cols(1 - core)]
    b_copy.start()
    core_sum(CHUNKS - 1)
    b_copy.wait_recv()
    y_send[...] = bucket[:, half_cols(core)] + b_recv[...]
    rows_copy = y_copy(y_send, y_recv, y_sem)
    rows_copy.start()
    finish(CHUNKS - 3)
    rows_copy.wait_recv()
    a_send[...] = y_send[...] + y_recv[...]

    def a_copy(step):
        to = (me + step) % 8
        return pltpu.make_async_remote_copy(
            src_ref=a_send.at[pl.ds(pl.multiple_of(to * SLOT, SLOT), SLOT), :],
            dst_ref=a_recv.at[me],
            send_sem=a_send_sem.at[step],
            recv_sem=a_recv_sem.at[me],
            device_id=(dp, to),
            device_id_type=MESH,
        )

    def a_arrived(step):
        origin = (me + 8 - step) % 8
        return pltpu.make_async_remote_copy(
            src_ref=a_send.at[pl.ds(0, SLOT), :],
            dst_ref=a_recv.at[origin],
            send_sem=a_send_sem.at[step],
            recv_sem=a_recv_sem.at[origin],
            device_id=(dp, origin),
            device_id_type=MESH,
        )

    for step in range(1, 8):
        a_copy(step).start()
    a_recv[me] = a_send[pl.ds(pl.multiple_of(me * SLOT, SLOT), SLOT), :]
    finish(CHUNKS - 2)
    for step in range(1, 8):
        a_arrived(step).wait_recv()
    h_copy = sibling_copy(a_recv, sib_recv, h_sem)
    h_copy.start()
    finish(CHUNKS - 1)
    h_copy.wait_recv()
    for t in range(8):
        for k in range(2):
            at = (t % 2) * 2 * half + k * half
            grads_out[t // 2, :, at : at + half] = jnp.where(core == k, a_recv[t], sib_recv[t])

    h_copy.wait_send()
    b_copy.wait_send()
    rows_copy.wait_send()
    for step in range(1, 8):
        a_copy(step).wait_send()

    def sent(copy):
        copy.wait_send()

    def drain(c, carry):
        each_own(c, sent)
        for far in (1, 2, 3):
            each_forward(c, far, sent, False)
        each_relay(c, sent, False)
        part_copy(c).wait_send()
        q_copy(c).wait_send()
        s_copy(c).wait_send()
        final_copy(c).wait()
        out_copy(c).wait()
        return carry

    lax.fori_loop(0, CHUNKS, drain, 0)


def fused(
    embedded,
    resid_grad,
    query_grad,
    query_weight,
    ngram_rows,
    touched_rows,
    row_values,
    row_mean,
    row_square,
):
    micro, group, width = embedded.shape
    hidden = query_grad.shape[2]
    tables = touched_rows.shape[0]
    table_idx = lax.axis_index("table")
    slice_idx = table_idx * width // SW
    entries = touched_rows.shape[2]
    ids = lax.dynamic_index_in_dim(ngram_rows, slice_idx, 2, False).reshape(1, micro * group)
    listed = lax.dynamic_index_in_dim(touched_rows, slice_idx, 1, False)
    listed = jnp.pad(listed, ((0, 0), (0, SLOT - entries)), constant_values=-1).reshape(tables * SLOT, 1)
    onehot = (listed == ids).astype(jnp.bfloat16)

    cols, half, rows = hidden // CHUNKS, width // 2, width // 2
    slots = tables * SLOT
    f32, bf16, i16 = jnp.float32, jnp.bfloat16, jnp.int16
    dma = pltpu.SemaphoreType.DMA
    vmem = pltpu.VMEM
    anywhere = pl.BlockSpec(memory_space=pl.ANY)
    in_vmem = pl.BlockSpec(memory_space=pltpu.VMEM)
    weight_grad, grads = pl.pallas_call(
        kernel,
        out_shape=(
            jax.ShapeDtypeStruct((width, hidden), f32),
            jax.ShapeDtypeStruct((SLICES, SLOT, SW), f32),
        ),
        in_specs=[anywhere] * 4 + [in_vmem],
        out_specs=(anywhere, in_vmem),
        scratch_shapes=[
            vmem((micro, group, width), bf16),
            vmem((width, micro * group), bf16),
            vmem((micro, group, width), bf16),
            vmem((width, hidden), bf16),
            vmem((CHUNKS, micro, group, cols), bf16),
            vmem((CHUNKS, rows, cols), f32),
            vmem((CHUNKS, rows, cols), f32),
            vmem((CHUNKS, rows, cols), f32),
            vmem((CHUNKS, rows, cols), i16),
            vmem((CHUNKS, rows, cols), i16),
            vmem((CHUNKS, 8, cols), f32),
            vmem((CHUNKS, 8, cols), f32),
            vmem((CHUNKS, rows, cols), f32),
            vmem((slots, width), f32),
            vmem((slots, half), f32),
            vmem((slots, half), f32),
            vmem((slots, half), f32),
            vmem((slots, half), f32),
            vmem((slots, half), f32),
            vmem((tables, SLOT, half), f32),
            vmem((tables, SLOT, half), f32),
            dma((3 + CHUNKS,)),
            dma((CHUNKS, tables, 3)),
            dma((CHUNKS, tables)),
            dma((CHUNKS, 2)),
            dma((CHUNKS, 2)),
            dma((CHUNKS, 2)),
            dma((CHUNKS, 2)),
            dma((CHUNKS,)),
            dma((2,)),
            dma((2,)),
            dma((tables,)),
            dma((tables,)),
            dma((2,)),
        ],
        compiler_params=pltpu.CompilerParams(
            collective_id=0, has_side_effects=True, vmem_limit_bytes=40 * 1024 * 1024
        ),
        cost_estimate=pl.CostEstimate(flops=3 * 10**9, bytes_accessed=2 * 10**7, transcendentals=0),
    )(embedded, resid_grad, query_grad, query_weight, onehot)

    mine = lax.dynamic_index_in_dim(touched_rows, table_idx, 0, False)
    live = (mine >= 0)[..., None]
    values_next, mean_next, square_next = adam_rows(
        grads[:, :entries], row_values[0], row_mean[0], row_square[0], live
    )
    return (weight_grad, values_next[None], mean_next[None], square_next[None])


def solution(mesh):
    placed = (
        P(None, "dp", "table"),
        P(None, "dp", "table"),
        P(None, ("dp", "table"), None),
        P("table", None),
        P(None, "dp", None),
        P(),
        P("table", None, None, None),
        P("table", None, None, None),
        P("table", None, None, None),
    )
    fits = mesh.shape["dp"] == 4 and mesh.shape["table"] == 8
    return jax.shard_map(
        fused if fits else local,
        mesh=mesh,
        in_specs=placed,
        out_specs=(
            P("table", None),
            P("table", None, None, None),
            P("table", None, None, None),
            P("table", None, None, None),
        ),
        check_vma=False,
    )
```

```python
import functools

import jax
import jax.numpy as jnp
from jax import lax
from jax.experimental import pallas as pl
from jax.experimental.pallas import tpu as pltpu
from jax.sharding import PartitionSpec as P

SLICES = 4
SW = 1024


beta_one = 0.9
beta_two = 0.95
learn_rate = 0.01
adam_eps = 1e-08
adam_step = 10


def adam_rows(grads, values, mean, square, live):
    corr_one = 1.0 - beta_one**adam_step
    corr_two = 1.0 - beta_two**adam_step
    mean_next = beta_one * mean + (1.0 - beta_one) * grads
    square_next = beta_two * square + (1.0 - beta_two) * grads * grads
    update = learn_rate * (mean_next / corr_one) / (jnp.sqrt(square_next / corr_two) + adam_eps)
    values_next = values - update
    return (
        jnp.where(live, values_next, values),
        jnp.where(live, mean_next, mean),
        jnp.where(live, square_next, square),
    )


def make_step(emb_part, weight_part, carry, piece):
    back_part, wgrad = carry
    back = jnp.einsum("mrh,ph->mrp", piece, weight_part, preferred_element_type=jnp.float32)
    back_part = back
    wgrad = wgrad + jnp.einsum("mrp,mrh->ph", emb_part, piece, preferred_element_type=jnp.float32)
    return (back_part, wgrad)


def local(
    embedded,
    resid_grad,
    query_grad,
    query_weight,
    ngram_rows,
    touched_rows,
    row_values,
    row_mean,
    row_square,
):
    micro_count, group_tokens, width_part = embedded.shape
    hidden = query_grad.shape[2]
    tables = lax.axis_size("table")
    table_idx = lax.axis_index("table")
    zero_grad = jnp.zeros((width_part, hidden), jnp.float32)
    wgrad = zero_grad
    backs = []
    for micro in range(micro_count):
        start_back = jnp.zeros((1, group_tokens, width_part), jnp.float32)
        back_one, wgrad = make_step(
            embedded[micro : micro + 1],
            query_weight,
            (start_back, wgrad),
            lax.all_gather(query_grad[micro : micro + 1], "table", axis=1, tiled=True),
        )
        backs.append(back_one)
    back_all = jnp.concatenate(backs, axis=0)
    emb_grad = resid_grad.astype(jnp.float32) + back_all
    weight_grad = lax.psum(wgrad, "dp")
    slice_idx = table_idx * width_part // SW
    ids = lax.dynamic_index_in_dim(ngram_rows, slice_idx, 2, False)
    listed = lax.dynamic_index_in_dim(touched_rows, slice_idx, 1, False)
    entries = listed.shape[1]
    flat_list = listed.reshape(tables * entries)
    onehot = (ids[:, :, None] == flat_list[None, None, :]).astype(jnp.float32)
    buckets = jnp.einsum(
        "mtk,mtp->kp",
        onehot,
        emb_grad,
        precision=lax.Precision.HIGHEST,
        preferred_element_type=jnp.float32,
    )
    buckets = buckets.reshape(tables, entries, width_part)
    arrived = lax.all_to_all(buckets, "table", split_axis=0, concat_axis=0, tiled=True)
    per_slice = tables // SLICES
    local_grad = (
        arrived.reshape(SLICES, per_slice, entries, width_part)
        .transpose(0, 2, 1, 3)
        .reshape(SLICES, entries, per_slice * width_part)
    )
    mine = lax.dynamic_index_in_dim(touched_rows, table_idx, 0, False)
    live = (mine >= 0)[..., None]
    values = row_values[0]
    mean = row_mean[0]
    square = row_square[0]
    grads = lax.psum(local_grad, "dp")
    values_next, mean_next, square_next = adam_rows(grads, values, mean, square, live)
    return (weight_grad, values_next[None], mean_next[None], square_next[None])


CHUNKS = 8
SLOT = 16
MESH = pl.DeviceIdType.MESH
UP, DOWN, ACROSS = 0, 1, 2


def kernel(
    emb_hbm,
    resid_hbm,
    qg_hbm,
    w_hbm,
    ids_hbm,
    touched_hbm,
    out_hbm,
    grads_out,
    live_out,
    ids,
    touched,
    lists,
    onehot,
    emb,
    emb_t,
    resid,
    w,
    gq,
    part_own,
    part_send,
    part_recv,
    q_send,
    q_recv,
    s_send,
    s_recv,
    res,
    bucket,
    b_send,
    b_recv,
    y_send,
    y_recv,
    a_send,
    a_recv,
    sib_recv,
    load_sem,
    g_send_sem,
    g_recv_sem,
    p_sem,
    q_sem,
    s_sem,
    f_sem,
    o_sem,
    b_sem,
    y_sem,
    a_send_sem,
    a_recv_sem,
    h_sem,
):
    dp, me = lax.axis_index("dp"), lax.axis_index("table")
    y, core = dp // 2, dp % 2
    z, x = me // 2, me % 2
    sib = dp + 1 - 2 * core
    ynb = (1 - y) * 2 + core
    zpair = z + 1 - 2 * (z % 2)
    micro, mine, hidden = qg_hbm.shape
    cols = hidden // CHUNKS
    rows = emb_t.shape[0] // 2

    barrier = pltpu.get_barrier_semaphore()
    for step in range(1, 8):
        pl.semaphore_signal(barrier, inc=1, device_id=(dp, (me + step) % 8), device_id_type=MESH)
    pl.semaphore_signal(barrier, inc=1, device_id=(sib, me), device_id_type=MESH)
    pl.semaphore_signal(barrier, inc=1, device_id=(ynb, me), device_id_type=MESH)

    loads = [
        pltpu.make_async_copy(emb_hbm, emb, load_sem.at[0]),
        pltpu.make_async_copy(resid_hbm, resid, load_sem.at[1]),
        pltpu.make_async_copy(w_hbm, w, load_sem.at[2]),
        pltpu.make_async_copy(ids_hbm, ids, load_sem.at[3]),
        pltpu.make_async_copy(touched_hbm, touched, load_sem.at[4]),
    ]

    def span(c):
        return pl.ds(pl.multiple_of(c * cols, cols), cols)

    def tokens(t):
        return pl.ds(pl.multiple_of(t * mine, mine), mine)

    def held(c, t):
        return gq.at[c, :, tokens(t), :]

    def own_load(c):
        return pltpu.make_async_copy(qg_hbm.at[:, :, span(c)], held(c, me), load_sem.at[5 + c])

    pl.semaphore_wait(barrier, 9)

    def shard_copy(c, t, way, source=None):
        to_z = z + 1 if way == UP else z - 1
        to = (dp, to_z * 2 + x) if way != ACROSS else (dp, z * 2 + 1 - x)
        return pltpu.make_async_remote_copy(
            src_ref=held(c, t) if source is None else source,
            dst_ref=held(c, t),
            send_sem=g_send_sem.at[c, t, way],
            recv_sem=g_recv_sem.at[c, t],
            device_id=to,
            device_id_type=MESH,
        )

    def arrived(c, t):
        shard_copy(c, t, ACROSS).wait_recv()

    def each_own(c, act):
        own = qg_hbm.at[:, :, span(c)]

        @pl.when(z < 3)
        def _():
            act(shard_copy(c, me, UP, own))

        @pl.when(z > 0)
        def _():
            act(shard_copy(c, me, DOWN, own))

        act(shard_copy(c, me, ACROSS, own))

    def each_forward(c, far, act, wait):
        for sign, way in ((-1, UP), (1, DOWN)):
            from_z = z + sign * far
            t = from_z * 2 + x
            there = from_z >= 0 if sign < 0 else from_z < 4
            onward = z < 3 if way == UP else z > 0

            @pl.when(there)
            def _():
                if wait:
                    arrived(c, t)

                @pl.when(onward)
                def _():
                    act(shard_copy(c, t, way))

                if far == 1:

                    @pl.when((c % 2 == 0) | (from_z != zpair))
                    def _():
                        act(shard_copy(c, t, ACROSS))
                else:
                    act(shard_copy(c, t, ACROSS))

    def each_relay(c, act, wait):
        t = z * 2 + 1 - x

        @pl.when(c % 2 == 1)
        def _():
            if wait:
                arrived(c, t)

            @pl.when(z % 2 == 0)
            def _():
                act(shard_copy(c, t, UP))

            @pl.when(z % 2 == 1)
            def _():
                act(shard_copy(c, t, DOWN))

    def start(copy):
        copy.start()

    def sibling_copy(src, dst, sems):
        return pltpu.make_async_remote_copy(
            src_ref=src, dst_ref=dst, send_sem=sems.at[0], recv_sem=sems.at[1], device_id=(sib, me), device_id_type=MESH
        )

    def y_copy(src, dst, sems):
        return pltpu.make_async_remote_copy(
            src_ref=src, dst_ref=dst, send_sem=sems.at[0], recv_sem=sems.at[1], device_id=(ynb, me), device_id_type=MESH
        )

    def part_copy(c):
        return sibling_copy(part_send.at[c], part_recv.at[c], p_sem.at[c])

    def q_copy(c):
        return y_copy(q_send.at[c], q_recv.at[c], q_sem.at[c])

    def s_copy(c):
        return y_copy(s_send.at[c], s_recv.at[c], s_sem.at[c])

    def out_rows(k):
        return pl.ds(pl.multiple_of(k * rows, rows), rows)

    def final_copy(c):
        return sibling_copy(res.at[c], out_hbm.at[out_rows(core), span(c)], f_sem.at[c])

    def out_copy(c):
        return pltpu.make_async_copy(res.at[c], out_hbm.at[out_rows(core), span(c)], o_sem.at[c])

    def dot(a, b):
        return jnp.dot(a, b, preferred_element_type=jnp.float32)

    def dot_nt(a, b):
        return lax.dot_general(a, b, (((1,), (1,)), ((), ())), preferred_element_type=jnp.float32)

    def compute(c, between=None):
        for far in (1, 2, 3):
            other = (z + far) % 4
            arrived(c, other * 2 + 1 - x)

        @pl.when(c % 2 == 0)
        def _():
            arrived(c, z * 2 + 1 - x)

        own_load(c).wait()
        block = gq[c].reshape(micro * mine * 8, cols)
        sums = dot(onehot[...], block)
        high = sums.astype(jnp.bfloat16)
        rest = sums - high.astype(jnp.float32)
        mid = rest.astype(jnp.bfloat16)
        low = (rest - mid.astype(jnp.float32)).astype(jnp.bfloat16)
        w_part = w[:, span(c)]
        bucket[...] += dot_nt(high, w_part) + dot_nt(mid, w_part) + dot_nt(low, w_part)
        if between is not None:
            between()
        part_send[c] = dot(emb_t[out_rows(1 - core), :], block)
        part_copy(c).start()
        part_own[c] = dot(emb_t[out_rows(core), :], block)

    def core_sum(c):
        part_copy(c).wait_recv()
        total = part_own[c] + part_recv[c]
        top = jnp.maximum(jnp.max(jnp.abs(total), axis=0, keepdims=True), 1e-30)
        codes = jnp.round(total * (32767.0 / top))
        q_send[c] = codes.astype(jnp.int32).astype(jnp.int16)
        s_send[c] = jnp.broadcast_to(top * (1.0 / 32767.0), s_send.shape[1:])
        q_copy(c).start()
        s_copy(c).start()

    def finish(c):
        q_copy(c).wait_recv()
        s_copy(c).wait_recv()
        here = q_send[c].astype(jnp.int32).astype(jnp.float32) * s_send[c][0:1, :]
        there = q_recv[c].astype(jnp.int32).astype(jnp.float32) * s_recv[c][0:1, :]
        res[c] = jnp.where(y == 0, here, there) + jnp.where(y == 0, there, here)
        final_copy(c).start()
        out_copy(c).start()

    def guarded(c, stage):
        @pl.when((c >= 0) & (c < CHUNKS))
        def _():
            stage(c)

    def forward_stage(far):
        def stage(c):
            each_forward(c, far, start, True)
            if far == 1:
                each_relay(c, start, True)

        return stage

    for c in range(2):
        each_own(c, start)
    for at in (4, 3, 1, 0, 2):
        loads[at].start()
    for c in range(CHUNKS):
        own_load(c).start()

    group = mine * 8
    width = emb_t.shape[0]
    entries = touched.shape[2]
    slice_idx = me * width // SW
    loads[4].wait()
    lists[...] = jnp.full(lists.shape, -1.0, jnp.float32)
    listed = touched[:, 0, :]
    for s in range(1, SLICES):
        listed = jnp.where(slice_idx == s, touched[:, s, :], listed)
    lists[0:8, 0:entries] = listed.astype(jnp.float32)
    lists[8 : 8 + SLICES, 0:entries] = touched[me].astype(jnp.float32)
    columns = lists[...].T
    for s in range(SLICES):
        live_out[:, s, :] = jnp.broadcast_to(columns[0:entries, 8 + s : 9 + s], (entries, live_out.shape[2]))
    loads[3].wait()
    for m in range(micro):
        row = ids[m, pl.ds(slice_idx, 1), :].astype(jnp.float32)
        for o in range(8):
            hit = columns[0:SLOT, o : o + 1] == row
            onehot[o * SLOT : (o + 1) * SLOT, m * group : (m + 1) * group] = jnp.where(hit, 1.0, 0.0).astype(jnp.bfloat16)
    loads[1].wait()
    bucket[...] = dot(onehot[:, 0:group], resid[0]) + dot(onehot[:, group : 2 * group], resid[1])
    loads[0].wait()
    for m in range(micro):
        emb_t[:, m * group : (m + 1) * group] = emb[m].T
    loads[2].wait()

    def slot(s, carry):
        guarded(s, lambda c: each_own(c, start))
        guarded(s - 2, forward_stage(1))
        guarded(s - 3, forward_stage(2))
        guarded(s - 4, forward_stage(3))
        guarded(s - 5, compute)
        guarded(s - 6, core_sum)
        guarded(s - 8, finish)
        return carry

    lax.fori_loop(2, CHUNKS + 4, slot, 0)

    half = b_send.shape[1]

    def half_cols(k):
        return pl.ds(pl.multiple_of(k * half, half), half)

    b_copy = sibling_copy(b_send, b_recv, b_sem)

    def send_bucket():
        b_send[...] = bucket[:, half_cols(1 - core)]
        b_copy.start()

    compute(CHUNKS - 1, send_bucket)
    core_sum(CHUNKS - 2)
    b_copy.wait_recv()
    y_send[...] = bucket[:, half_cols(core)] + b_recv[...]
    rows_copy = y_copy(y_send, y_recv, y_sem)
    rows_copy.start()
    core_sum(CHUNKS - 1)
    finish(CHUNKS - 4)
    finish(CHUNKS - 3)
    rows_copy.wait_recv()
    a_send[...] = y_send[...] + y_recv[...]

    def a_copy(step):
        to = (me + step) % 8
        return pltpu.make_async_remote_copy(
            src_ref=a_send.at[pl.ds(pl.multiple_of(to * SLOT, SLOT), SLOT), :],
            dst_ref=a_recv.at[me],
            send_sem=a_send_sem.at[step],
            recv_sem=a_recv_sem.at[me],
            device_id=(dp, to),
            device_id_type=MESH,
        )

    def a_arrived(step):
        origin = (me + 8 - step) % 8
        return pltpu.make_async_remote_copy(
            src_ref=a_send.at[pl.ds(0, SLOT), :],
            dst_ref=a_recv.at[origin],
            send_sem=a_send_sem.at[step],
            recv_sem=a_recv_sem.at[origin],
            device_id=(dp, origin),
            device_id_type=MESH,
        )

    for step in range(1, 8):
        a_copy(step).start()
    a_recv[me] = a_send[pl.ds(pl.multiple_of(me * SLOT, SLOT), SLOT), :]
    finish(CHUNKS - 2)
    for step in range(1, 8):
        a_arrived(step).wait_recv()
    h_copy = sibling_copy(a_recv, sib_recv, h_sem)
    h_copy.start()
    finish(CHUNKS - 1)
    h_copy.wait_recv()
    for t in range(8):
        for k in range(2):
            at = (t % 2) * 2 * half + k * half
            piece = jnp.where(core == k, a_recv[t], sib_recv[t])
            grads_out[:, t // 2, at : at + half] = piece[0:entries]

    h_copy.wait_send()
    b_copy.wait_send()
    rows_copy.wait_send()
    for step in range(1, 8):
        a_copy(step).wait_send()

    def sent(copy):
        copy.wait_send()

    def drain(c, carry):
        each_own(c, sent)
        for far in (1, 2, 3):
            each_forward(c, far, sent, False)
        each_relay(c, sent, False)
        part_copy(c).wait_send()
        q_copy(c).wait_send()
        s_copy(c).wait_send()
        final_copy(c).wait()
        out_copy(c).wait()
        return carry

    lax.fori_loop(0, CHUNKS, drain, 0)


def fused(
    embedded,
    resid_grad,
    query_grad,
    query_weight,
    ngram_rows,
    touched_rows,
    row_values,
    row_mean,
    row_square,
):
    micro, group, width = embedded.shape
    hidden = query_grad.shape[2]
    tables = touched_rows.shape[0]
    entries = touched_rows.shape[2]
    cols, half, rows = hidden // CHUNKS, width // 2, width // 2
    slots = tables * SLOT
    f32, bf16, i16 = jnp.float32, jnp.bfloat16, jnp.int16
    dma = pltpu.SemaphoreType.DMA
    vmem = pltpu.VMEM
    anywhere = pl.BlockSpec(memory_space=pl.ANY)
    in_hbm = pl.BlockSpec(memory_space=pltpu.HBM)
    in_vmem = pl.BlockSpec(memory_space=pltpu.VMEM)
    operands = (embedded, resid_grad, query_grad, query_weight, ngram_rows.transpose(0, 2, 1), touched_rows)
    operands = [pltpu.with_memory_space_constraint(operand, pltpu.HBM) for operand in operands]
    weight_grad, grads, lists = pl.pallas_call(
        kernel,
        out_shape=(
            jax.ShapeDtypeStruct((width, hidden), f32),
            jax.ShapeDtypeStruct((entries, SLICES, SW), f32),
            jax.ShapeDtypeStruct((entries, SLICES, SW), f32),
        ),
        in_specs=[in_hbm] * 6,
        out_specs=(anywhere, in_vmem, in_vmem),
        scratch_shapes=[
            vmem((micro, SLICES, group), jnp.int32),
            vmem(touched_rows.shape, jnp.int32),
            vmem((128, 128), f32),
            vmem((slots, micro * group), bf16),
            vmem((micro, group, width), bf16),
            vmem((width, micro * group), bf16),
            vmem((micro, group, width), bf16),
            vmem((width, hidden), bf16),
            vmem((CHUNKS, micro, group, cols), bf16),
            vmem((CHUNKS, rows, cols), f32),
            vmem((CHUNKS, rows, cols), f32),
            vmem((CHUNKS, rows, cols), f32),
            vmem((CHUNKS, rows, cols), i16),
            vmem((CHUNKS, rows, cols), i16),
            vmem((CHUNKS, 8, cols), f32),
            vmem((CHUNKS, 8, cols), f32),
            vmem((CHUNKS, rows, cols), f32),
            vmem((slots, width), f32),
            vmem((slots, half), f32),
            vmem((slots, half), f32),
            vmem((slots, half), f32),
            vmem((slots, half), f32),
            vmem((slots, half), f32),
            vmem((tables, SLOT, half), f32),
            vmem((tables, SLOT, half), f32),
            dma((5 + CHUNKS,)),
            dma((CHUNKS, tables, 3)),
            dma((CHUNKS, tables)),
            dma((CHUNKS, 2)),
            dma((CHUNKS, 2)),
            dma((CHUNKS, 2)),
            dma((CHUNKS, 2)),
            dma((CHUNKS,)),
            dma((2,)),
            dma((2,)),
            dma((tables,)),
            dma((tables,)),
            dma((2,)),
        ],
        compiler_params=pltpu.CompilerParams(
            collective_id=0, has_side_effects=True, vmem_limit_bytes=40 * 1024 * 1024
        ),
        cost_estimate=pl.CostEstimate(flops=3 * 10**9, bytes_accessed=2 * 10**7, transcendentals=0),
    )(*operands)

    def turned(rows):
        return rows[0].transpose(1, 0, 2)

    after = adam_rows(grads, turned(row_values), turned(row_mean), turned(row_square), lists >= 0)
    values_next, mean_next, square_next = [rows.transpose(1, 0, 2)[None] for rows in after]
    return (weight_grad, values_next, mean_next, square_next)


def solution(mesh):
    placed = (
        P(None, "dp", "table"),
        P(None, "dp", "table"),
        P(None, ("dp", "table"), None),
        P("table", None),
        P(None, "dp", None),
        P(),
        P("table", None, None, None),
        P("table", None, None, None),
        P("table", None, None, None),
    )
    fits = mesh.shape["dp"] == 4 and mesh.shape["table"] == 8
    return jax.shard_map(
        fused if fits else local,
        mesh=mesh,
        in_specs=placed,
        out_specs=(
            P("table", None),
            P("table", None, None, None),
            P("table", None, None, None),
            P("table", None, None, None),
        ),
        check_vma=False,
    )
```

```python
import functools

import jax
import jax.numpy as jnp
from jax import lax
from jax.experimental import pallas as pl
from jax.experimental.pallas import tpu as pltpu
from jax.sharding import PartitionSpec as P

SLICES = 4
SW = 1024


beta_one = 0.9
beta_two = 0.95
learn_rate = 0.01
adam_eps = 1e-08
adam_step = 10


def adam_rows(grads, values, mean, square, live):
    corr_one = 1.0 - beta_one**adam_step
    corr_two = 1.0 - beta_two**adam_step
    mean_next = beta_one * mean + (1.0 - beta_one) * grads
    square_next = beta_two * square + (1.0 - beta_two) * grads * grads
    update = learn_rate * (mean_next / corr_one) / (jnp.sqrt(square_next / corr_two) + adam_eps)
    values_next = values - update
    return (
        jnp.where(live, values_next, values),
        jnp.where(live, mean_next, mean),
        jnp.where(live, square_next, square),
    )


def make_step(emb_part, weight_part, carry, piece):
    back_part, wgrad = carry
    back = jnp.einsum("mrh,ph->mrp", piece, weight_part, preferred_element_type=jnp.float32)
    back_part = back
    wgrad = wgrad + jnp.einsum("mrp,mrh->ph", emb_part, piece, preferred_element_type=jnp.float32)
    return (back_part, wgrad)


def local(
    embedded,
    resid_grad,
    query_grad,
    query_weight,
    ngram_rows,
    touched_rows,
    row_values,
    row_mean,
    row_square,
):
    micro_count, group_tokens, width_part = embedded.shape
    hidden = query_grad.shape[2]
    tables = lax.axis_size("table")
    table_idx = lax.axis_index("table")
    zero_grad = jnp.zeros((width_part, hidden), jnp.float32)
    wgrad = zero_grad
    backs = []
    for micro in range(micro_count):
        start_back = jnp.zeros((1, group_tokens, width_part), jnp.float32)
        back_one, wgrad = make_step(
            embedded[micro : micro + 1],
            query_weight,
            (start_back, wgrad),
            lax.all_gather(query_grad[micro : micro + 1], "table", axis=1, tiled=True),
        )
        backs.append(back_one)
    back_all = jnp.concatenate(backs, axis=0)
    emb_grad = resid_grad.astype(jnp.float32) + back_all
    weight_grad = lax.psum(wgrad, "dp")
    slice_idx = table_idx * width_part // SW
    ids = lax.dynamic_index_in_dim(ngram_rows, slice_idx, 2, False)
    listed = lax.dynamic_index_in_dim(touched_rows, slice_idx, 1, False)
    entries = listed.shape[1]
    flat_list = listed.reshape(tables * entries)
    onehot = (ids[:, :, None] == flat_list[None, None, :]).astype(jnp.float32)
    buckets = jnp.einsum(
        "mtk,mtp->kp",
        onehot,
        emb_grad,
        precision=lax.Precision.HIGHEST,
        preferred_element_type=jnp.float32,
    )
    buckets = buckets.reshape(tables, entries, width_part)
    arrived = lax.all_to_all(buckets, "table", split_axis=0, concat_axis=0, tiled=True)
    per_slice = tables // SLICES
    local_grad = (
        arrived.reshape(SLICES, per_slice, entries, width_part)
        .transpose(0, 2, 1, 3)
        .reshape(SLICES, entries, per_slice * width_part)
    )
    mine = lax.dynamic_index_in_dim(touched_rows, table_idx, 0, False)
    live = (mine >= 0)[..., None]
    values = row_values[0]
    mean = row_mean[0]
    square = row_square[0]
    grads = lax.psum(local_grad, "dp")
    values_next, mean_next, square_next = adam_rows(grads, values, mean, square, live)
    return (weight_grad, values_next[None], mean_next[None], square_next[None])


CHUNKS = 8
SLOT = 16
MESH = pl.DeviceIdType.MESH
UP, DOWN, ACROSS = 0, 1, 2


def kernel(
    emb_hbm,
    resid_hbm,
    qg_hbm,
    w_hbm,
    ids_hbm,
    touched_hbm,
    out_hbm,
    grads_out,
    live_out,
    ids,
    touched,
    lists,
    onehot,
    emb,
    emb_t,
    resid,
    w,
    gq,
    part_own,
    part_send,
    part_recv,
    q_send,
    q_recv,
    s_send,
    s_recv,
    res,
    bucket,
    b_send,
    b_recv,
    y_send,
    y_recv,
    a_send,
    a_recv,
    sib_recv,
    load_sem,
    g_send_sem,
    g_recv_sem,
    p_sem,
    q_sem,
    s_sem,
    f_sem,
    o_sem,
    b_sem,
    y_sem,
    a_send_sem,
    a_recv_sem,
    h_sem,
):
    dp, me = lax.axis_index("dp"), lax.axis_index("table")
    y, core = dp // 2, dp % 2
    z, x = me // 2, me % 2
    sib = dp + 1 - 2 * core
    ynb = (1 - y) * 2 + core
    zpair = z + 1 - 2 * (z % 2)
    micro, mine, hidden = qg_hbm.shape
    cols = hidden // CHUNKS
    rows = emb_t.shape[0] // 2

    barrier = pltpu.get_barrier_semaphore()
    for step in range(1, 8):
        pl.semaphore_signal(barrier, inc=1, device_id=(dp, (me + step) % 8), device_id_type=MESH)
    pl.semaphore_signal(barrier, inc=1, device_id=(sib, me), device_id_type=MESH)
    pl.semaphore_signal(barrier, inc=1, device_id=(ynb, me), device_id_type=MESH)

    loads = [
        pltpu.make_async_copy(emb_hbm, emb, load_sem.at[0]),
        pltpu.make_async_copy(resid_hbm, resid, load_sem.at[1]),
        pltpu.make_async_copy(w_hbm, w, load_sem.at[2]),
        pltpu.make_async_copy(ids_hbm, ids, load_sem.at[3]),
        pltpu.make_async_copy(touched_hbm, touched, load_sem.at[4]),
    ]

    def span(c):
        return pl.ds(pl.multiple_of(c * cols, cols), cols)

    def tokens(t):
        return pl.ds(pl.multiple_of(t * mine, mine), mine)

    def held(c, t):
        return gq.at[c, :, tokens(t), :]

    def own_load(c):
        return pltpu.make_async_copy(qg_hbm.at[:, :, span(c)], held(c, me), load_sem.at[5 + c])

    pl.semaphore_wait(barrier, 9)

    def shard_copy(c, t, way, source=None):
        to_z = z + 1 if way == UP else z - 1
        to = (dp, to_z * 2 + x) if way != ACROSS else (dp, z * 2 + 1 - x)
        return pltpu.make_async_remote_copy(
            src_ref=held(c, t) if source is None else source,
            dst_ref=held(c, t),
            send_sem=g_send_sem.at[c, t, way],
            recv_sem=g_recv_sem.at[c, t],
            device_id=to,
            device_id_type=MESH,
        )

    def arrived(c, t):
        shard_copy(c, t, ACROSS).wait_recv()

    def each_own(c, act):
        own = qg_hbm.at[:, :, span(c)]

        @pl.when(z < 3)
        def _():
            act(shard_copy(c, me, UP, own))

        @pl.when(z > 0)
        def _():
            act(shard_copy(c, me, DOWN, own))

        act(shard_copy(c, me, ACROSS, own))

    def each_forward(c, far, act, wait):
        for sign, way in ((-1, UP), (1, DOWN)):
            from_z = z + sign * far
            t = from_z * 2 + x
            there = from_z >= 0 if sign < 0 else from_z < 4
            onward = z < 3 if way == UP else z > 0

            @pl.when(there)
            def _():
                if wait:
                    arrived(c, t)

                @pl.when(onward)
                def _():
                    act(shard_copy(c, t, way))

                if far == 1:

                    @pl.when((c % 2 == 0) | (from_z != zpair))
                    def _():
                        act(shard_copy(c, t, ACROSS))
                else:
                    act(shard_copy(c, t, ACROSS))

    def each_relay(c, act, wait):
        t = z * 2 + 1 - x

        @pl.when(c % 2 == 1)
        def _():
            if wait:
                arrived(c, t)

            @pl.when(z % 2 == 0)
            def _():
                act(shard_copy(c, t, UP))

            @pl.when(z % 2 == 1)
            def _():
                act(shard_copy(c, t, DOWN))

    def start(copy):
        copy.start()

    def sibling_copy(src, dst, sems):
        return pltpu.make_async_remote_copy(
            src_ref=src, dst_ref=dst, send_sem=sems.at[0], recv_sem=sems.at[1], device_id=(sib, me), device_id_type=MESH
        )

    def y_copy(src, dst, sems):
        return pltpu.make_async_remote_copy(
            src_ref=src, dst_ref=dst, send_sem=sems.at[0], recv_sem=sems.at[1], device_id=(ynb, me), device_id_type=MESH
        )

    def part_copy(c):
        return sibling_copy(part_send.at[c], part_recv.at[c], p_sem.at[c])

    def q_copy(c):
        return y_copy(q_send.at[c], q_recv.at[c], q_sem.at[c])

    def s_copy(c):
        return y_copy(s_send.at[c], s_recv.at[c], s_sem.at[c])

    def out_rows(k):
        return pl.ds(pl.multiple_of(k * rows, rows), rows)

    def final_copy(c):
        return sibling_copy(res.at[c], out_hbm.at[out_rows(core), span(c)], f_sem.at[c])

    def out_copy(c):
        return pltpu.make_async_copy(res.at[c], out_hbm.at[out_rows(core), span(c)], o_sem.at[c])

    def dot(a, b):
        return jnp.dot(a, b, preferred_element_type=jnp.float32)

    def dot_nt(a, b):
        return lax.dot_general(a, b, (((1,), (1,)), ((), ())), preferred_element_type=jnp.float32)

    def compute(c, between=None):
        for far in (1, 2, 3):
            other = (z + far) % 4
            arrived(c, other * 2 + 1 - x)

        @pl.when(c % 2 == 0)
        def _():
            arrived(c, z * 2 + 1 - x)

        own_load(c).wait()
        block = gq[c].reshape(micro * mine * 8, cols)
        sums = dot(onehot[...], block)
        high = sums.astype(jnp.bfloat16)
        rest = sums - high.astype(jnp.float32)
        mid = rest.astype(jnp.bfloat16)
        low = (rest - mid.astype(jnp.float32)).astype(jnp.bfloat16)
        w_part = w[:, span(c)]
        bucket[...] += dot_nt(high, w_part) + dot_nt(mid, w_part) + dot_nt(low, w_part)
        if between is not None:
            between()
        part_send[c] = dot(emb_t[out_rows(1 - core), :], block)
        part_copy(c).start()
        part_own[c] = dot(emb_t[out_rows(core), :], block)

    def core_sum(c):
        part_copy(c).wait_recv()
        total = part_own[c] + part_recv[c]
        top = jnp.maximum(jnp.max(jnp.abs(total), axis=0, keepdims=True), 1e-30)
        codes = jnp.round(total * (32767.0 / top))
        q_send[c] = codes.astype(jnp.int32).astype(jnp.int16)
        s_send[c] = jnp.broadcast_to(top * (1.0 / 32767.0), s_send.shape[1:])
        q_copy(c).start()
        s_copy(c).start()

    def finish(c):
        q_copy(c).wait_recv()
        s_copy(c).wait_recv()
        here = q_send[c].astype(jnp.int32).astype(jnp.float32) * s_send[c][0:1, :]
        there = q_recv[c].astype(jnp.int32).astype(jnp.float32) * s_recv[c][0:1, :]
        res[c] = jnp.where(y == 0, here, there) + jnp.where(y == 0, there, here)
        final_copy(c).start()
        out_copy(c).start()

    def guarded(c, stage):
        @pl.when((c >= 0) & (c < CHUNKS))
        def _():
            stage(c)

    def forward_stage(far):
        def stage(c):
            each_forward(c, far, start, True)
            if far == 1:
                each_relay(c, start, True)

        return stage

    for c in range(2):
        each_own(c, start)
    for at in (4, 3, 1, 0, 2):
        loads[at].start()
    for c in range(CHUNKS):
        own_load(c).start()

    group = mine * 8
    width = emb_t.shape[0]
    entries = touched.shape[2]
    slice_idx = me * width // SW
    loads[4].wait()
    lists[...] = jnp.full(lists.shape, -1.0, jnp.float32)
    listed = touched[:, 0, :]
    for s in range(1, SLICES):
        listed = jnp.where(slice_idx == s, touched[:, s, :], listed)
    lists[0:8, 0:entries] = listed.astype(jnp.float32)
    lists[8 : 8 + SLICES, 0:entries] = touched[me].astype(jnp.float32)
    columns = lists[...].T
    for s in range(SLICES):
        live_out[:, s, :] = jnp.broadcast_to(columns[0:entries, 8 + s : 9 + s], (entries, live_out.shape[2]))
    loads[3].wait()
    for m in range(micro):
        row = ids[m, pl.ds(slice_idx, 1), :].astype(jnp.float32)
        for o in range(8):
            hit = columns[0:SLOT, o : o + 1] == row
            onehot[o * SLOT : (o + 1) * SLOT, m * group : (m + 1) * group] = jnp.where(hit, 1.0, 0.0).astype(jnp.bfloat16)
    loads[1].wait()
    bucket[...] = dot(onehot[:, 0:group], resid[0]) + dot(onehot[:, group : 2 * group], resid[1])
    loads[0].wait()
    for m in range(micro):
        emb_t[:, m * group : (m + 1) * group] = emb[m].T
    loads[2].wait()

    def slot(s, carry):
        guarded(s, lambda c: each_own(c, start))
        guarded(s - 2, forward_stage(1))
        guarded(s - 4, forward_stage(2))
        guarded(s - 6, forward_stage(3))
        guarded(s - 8, compute)
        guarded(s - 9, core_sum)
        guarded(s - 10, finish)
        return carry

    lax.fori_loop(2, CHUNKS + 7, slot, 0)

    half = b_send.shape[1]

    def half_cols(k):
        return pl.ds(pl.multiple_of(k * half, half), half)

    b_copy = sibling_copy(b_send, b_recv, b_sem)

    def send_bucket():
        b_send[...] = bucket[:, half_cols(1 - core)]
        b_copy.start()

    compute(CHUNKS - 1, send_bucket)
    core_sum(CHUNKS - 2)
    b_copy.wait_recv()
    y_send[...] = bucket[:, half_cols(core)] + b_recv[...]
    rows_copy = y_copy(y_send, y_recv, y_sem)
    rows_copy.start()
    core_sum(CHUNKS - 1)
    finish(CHUNKS - 3)
    rows_copy.wait_recv()
    a_send[...] = y_send[...] + y_recv[...]

    def a_copy(step):
        to = (me + step) % 8
        return pltpu.make_async_remote_copy(
            src_ref=a_send.at[pl.ds(pl.multiple_of(to * SLOT, SLOT), SLOT), :],
            dst_ref=a_recv.at[me],
            send_sem=a_send_sem.at[step],
            recv_sem=a_recv_sem.at[me],
            device_id=(dp, to),
            device_id_type=MESH,
        )

    def a_arrived(step):
        origin = (me + 8 - step) % 8
        return pltpu.make_async_remote_copy(
            src_ref=a_send.at[pl.ds(0, SLOT), :],
            dst_ref=a_recv.at[origin],
            send_sem=a_send_sem.at[step],
            recv_sem=a_recv_sem.at[origin],
            device_id=(dp, origin),
            device_id_type=MESH,
        )

    for step in range(1, 8):
        a_copy(step).start()
    a_recv[me] = a_send[pl.ds(pl.multiple_of(me * SLOT, SLOT), SLOT), :]
    finish(CHUNKS - 2)
    for step in range(1, 8):
        a_arrived(step).wait_recv()
    h_copy = sibling_copy(a_recv, sib_recv, h_sem)
    h_copy.start()
    finish(CHUNKS - 1)
    h_copy.wait_recv()
    for t in range(8):
        for k in range(2):
            at = (t % 2) * 2 * half + k * half
            piece = jnp.where(core == k, a_recv[t], sib_recv[t])
            grads_out[:, t // 2, at : at + half] = piece[0:entries]

    h_copy.wait_send()
    b_copy.wait_send()
    rows_copy.wait_send()
    for step in range(1, 8):
        a_copy(step).wait_send()

    def sent(copy):
        copy.wait_send()

    def drain(c, carry):
        each_own(c, sent)
        for far in (1, 2, 3):
            each_forward(c, far, sent, False)
        each_relay(c, sent, False)
        part_copy(c).wait_send()
        q_copy(c).wait_send()
        s_copy(c).wait_send()
        final_copy(c).wait()
        out_copy(c).wait()
        return carry

    lax.fori_loop(0, CHUNKS, drain, 0)


def fused(
    embedded,
    resid_grad,
    query_grad,
    query_weight,
    ngram_rows,
    touched_rows,
    row_values,
    row_mean,
    row_square,
):
    micro, group, width = embedded.shape
    hidden = query_grad.shape[2]
    tables = touched_rows.shape[0]
    entries = touched_rows.shape[2]
    cols, half, rows = hidden // CHUNKS, width // 2, width // 2
    slots = tables * SLOT
    f32, bf16, i16 = jnp.float32, jnp.bfloat16, jnp.int16
    dma = pltpu.SemaphoreType.DMA
    vmem = pltpu.VMEM
    anywhere = pl.BlockSpec(memory_space=pl.ANY)
    in_hbm = pl.BlockSpec(memory_space=pltpu.HBM)
    in_vmem = pl.BlockSpec(memory_space=pltpu.VMEM)
    operands = (embedded, resid_grad, query_grad, query_weight, ngram_rows.transpose(0, 2, 1), touched_rows)
    operands = [pltpu.with_memory_space_constraint(operand, pltpu.HBM) for operand in operands]
    weight_grad, grads, lists = pl.pallas_call(
        kernel,
        out_shape=(
            jax.ShapeDtypeStruct((width, hidden), f32),
            jax.ShapeDtypeStruct((entries, SLICES, SW), f32),
            jax.ShapeDtypeStruct((entries, SLICES, SW), f32),
        ),
        in_specs=[in_hbm] * 6,
        out_specs=(anywhere, in_vmem, in_vmem),
        scratch_shapes=[
            vmem((micro, SLICES, group), jnp.int32),
            vmem(touched_rows.shape, jnp.int32),
            vmem((128, 128), f32),
            vmem((slots, micro * group), bf16),
            vmem((micro, group, width), bf16),
            vmem((width, micro * group), bf16),
            vmem((micro, group, width), bf16),
            vmem((width, hidden), bf16),
            vmem((CHUNKS, micro, group, cols), bf16),
            vmem((CHUNKS, rows, cols), f32),
            vmem((CHUNKS, rows, cols), f32),
            vmem((CHUNKS, rows, cols), f32),
            vmem((CHUNKS, rows, cols), i16),
            vmem((CHUNKS, rows, cols), i16),
            vmem((CHUNKS, 8, cols), f32),
            vmem((CHUNKS, 8, cols), f32),
            vmem((CHUNKS, rows, cols), f32),
            vmem((slots, width), f32),
            vmem((slots, half), f32),
            vmem((slots, half), f32),
            vmem((slots, half), f32),
            vmem((slots, half), f32),
            vmem((slots, half), f32),
            vmem((tables, SLOT, half), f32),
            vmem((tables, SLOT, half), f32),
            dma((5 + CHUNKS,)),
            dma((CHUNKS, tables, 3)),
            dma((CHUNKS, tables)),
            dma((CHUNKS, 2)),
            dma((CHUNKS, 2)),
            dma((CHUNKS, 2)),
            dma((CHUNKS, 2)),
            dma((CHUNKS,)),
            dma((2,)),
            dma((2,)),
            dma((tables,)),
            dma((tables,)),
            dma((2,)),
        ],
        compiler_params=pltpu.CompilerParams(
            collective_id=0, has_side_effects=True, vmem_limit_bytes=40 * 1024 * 1024
        ),
        cost_estimate=pl.CostEstimate(flops=3 * 10**9, bytes_accessed=2 * 10**7, transcendentals=0),
    )(*operands)

    def turned(rows):
        return rows[0].transpose(1, 0, 2)

    after = adam_rows(grads, turned(row_values), turned(row_mean), turned(row_square), lists >= 0)
    values_next, mean_next, square_next = [rows.transpose(1, 0, 2)[None] for rows in after]
    return (weight_grad, values_next, mean_next, square_next)


def solution(mesh):
    placed = (
        P(None, "dp", "table"),
        P(None, "dp", "table"),
        P(None, ("dp", "table"), None),
        P("table", None),
        P(None, "dp", None),
        P(),
        P("table", None, None, None),
        P("table", None, None, None),
        P("table", None, None, None),
    )
    fits = mesh.shape["dp"] == 4 and mesh.shape["table"] == 8
    return jax.shard_map(
        fused if fits else local,
        mesh=mesh,
        in_specs=placed,
        out_specs=(
            P("table", None),
            P("table", None, None, None),
            P("table", None, None, None),
            P("table", None, None, None),
        ),
        check_vma=False,
    )
```

```python
import functools

import jax
import jax.numpy as jnp
from jax import lax
from jax.experimental import pallas as pl
from jax.experimental.pallas import tpu as pltpu
from jax.sharding import PartitionSpec as P

SLICES = 4
SW = 1024


beta_one = 0.9
beta_two = 0.95
learn_rate = 0.01
adam_eps = 1e-08
adam_step = 10


def adam_rows(grads, values, mean, square, live):
    corr_one = 1.0 - beta_one**adam_step
    corr_two = 1.0 - beta_two**adam_step
    mean_next = beta_one * mean + (1.0 - beta_one) * grads
    square_next = beta_two * square + (1.0 - beta_two) * grads * grads
    update = learn_rate * (mean_next / corr_one) / (jnp.sqrt(square_next / corr_two) + adam_eps)
    values_next = values - update
    return (
        jnp.where(live, values_next, values),
        jnp.where(live, mean_next, mean),
        jnp.where(live, square_next, square),
    )


def make_step(emb_part, weight_part, carry, piece):
    back_part, wgrad = carry
    back = jnp.einsum("mrh,ph->mrp", piece, weight_part, preferred_element_type=jnp.float32)
    back_part = back
    wgrad = wgrad + jnp.einsum("mrp,mrh->ph", emb_part, piece, preferred_element_type=jnp.float32)
    return (back_part, wgrad)


def local(
    embedded,
    resid_grad,
    query_grad,
    query_weight,
    ngram_rows,
    touched_rows,
    row_values,
    row_mean,
    row_square,
):
    micro_count, group_tokens, width_part = embedded.shape
    hidden = query_grad.shape[2]
    tables = lax.axis_size("table")
    table_idx = lax.axis_index("table")
    zero_grad = jnp.zeros((width_part, hidden), jnp.float32)
    wgrad = zero_grad
    backs = []
    for micro in range(micro_count):
        start_back = jnp.zeros((1, group_tokens, width_part), jnp.float32)
        back_one, wgrad = make_step(
            embedded[micro : micro + 1],
            query_weight,
            (start_back, wgrad),
            lax.all_gather(query_grad[micro : micro + 1], "table", axis=1, tiled=True),
        )
        backs.append(back_one)
    back_all = jnp.concatenate(backs, axis=0)
    emb_grad = resid_grad.astype(jnp.float32) + back_all
    weight_grad = lax.psum(wgrad, "dp")
    slice_idx = table_idx * width_part // SW
    ids = lax.dynamic_index_in_dim(ngram_rows, slice_idx, 2, False)
    listed = lax.dynamic_index_in_dim(touched_rows, slice_idx, 1, False)
    entries = listed.shape[1]
    flat_list = listed.reshape(tables * entries)
    onehot = (ids[:, :, None] == flat_list[None, None, :]).astype(jnp.float32)
    buckets = jnp.einsum(
        "mtk,mtp->kp",
        onehot,
        emb_grad,
        precision=lax.Precision.HIGHEST,
        preferred_element_type=jnp.float32,
    )
    buckets = buckets.reshape(tables, entries, width_part)
    arrived = lax.all_to_all(buckets, "table", split_axis=0, concat_axis=0, tiled=True)
    per_slice = tables // SLICES
    local_grad = (
        arrived.reshape(SLICES, per_slice, entries, width_part)
        .transpose(0, 2, 1, 3)
        .reshape(SLICES, entries, per_slice * width_part)
    )
    mine = lax.dynamic_index_in_dim(touched_rows, table_idx, 0, False)
    live = (mine >= 0)[..., None]
    values = row_values[0]
    mean = row_mean[0]
    square = row_square[0]
    grads = lax.psum(local_grad, "dp")
    values_next, mean_next, square_next = adam_rows(grads, values, mean, square, live)
    return (weight_grad, values_next[None], mean_next[None], square_next[None])


LEAD = 4
CHUNKS = 8
SLOT = 16
MESH = pl.DeviceIdType.MESH
UP, DOWN, ACROSS = 0, 1, 2


def kernel(
    emb_hbm,
    resid_hbm,
    qg_hbm,
    w_hbm,
    ids_hbm,
    touched_hbm,
    out_hbm,
    grads_out,
    live_out,
    ids,
    touched,
    lists,
    onehot,
    emb,
    emb_t,
    resid,
    w,
    gq,
    part_own,
    part_send,
    part_recv,
    q_send,
    q_recv,
    s_send,
    s_recv,
    res,
    bucket,
    b_send,
    b_recv,
    y_send,
    y_recv,
    a_send,
    a_recv,
    sib_recv,
    load_sem,
    g_send_sem,
    g_recv_sem,
    p_sem,
    q_sem,
    s_sem,
    f_sem,
    o_sem,
    b_sem,
    y_sem,
    a_send_sem,
    a_recv_sem,
    h_sem,
):
    dp, me = lax.axis_index("dp"), lax.axis_index("table")
    y, core = dp // 2, dp % 2
    z, x = me // 2, me % 2
    sib = dp + 1 - 2 * core
    ynb = (1 - y) * 2 + core
    zpair = z + 1 - 2 * (z % 2)
    micro, mine, hidden = qg_hbm.shape
    cols = hidden // CHUNKS
    rows = emb_t.shape[0] // 2

    barrier = pltpu.get_barrier_semaphore()
    for step in range(1, 8):
        pl.semaphore_signal(barrier, inc=1, device_id=(dp, (me + step) % 8), device_id_type=MESH)
    pl.semaphore_signal(barrier, inc=1, device_id=(sib, me), device_id_type=MESH)
    pl.semaphore_signal(barrier, inc=1, device_id=(ynb, me), device_id_type=MESH)

    loads = [
        pltpu.make_async_copy(emb_hbm, emb, load_sem.at[0]),
        pltpu.make_async_copy(resid_hbm, resid, load_sem.at[1]),
        pltpu.make_async_copy(w_hbm, w, load_sem.at[2]),
        pltpu.make_async_copy(ids_hbm, ids, load_sem.at[3]),
        pltpu.make_async_copy(touched_hbm, touched, load_sem.at[4]),
    ]

    def span(c):
        return pl.ds(pl.multiple_of(c * cols, cols), cols)

    def tokens(t):
        return pl.ds(pl.multiple_of(t * mine, mine), mine)

    def held(c, t):
        return gq.at[c, :, tokens(t), :]

    def own_load(c):
        return pltpu.make_async_copy(qg_hbm.at[:, :, span(c)], held(c, me), load_sem.at[5 + c])

    pl.semaphore_wait(barrier, 9)

    def shard_copy(c, t, way, source=None):
        to_z = z + 1 if way == UP else z - 1
        to = (dp, to_z * 2 + x) if way != ACROSS else (dp, z * 2 + 1 - x)
        return pltpu.make_async_remote_copy(
            src_ref=held(c, t) if source is None else source,
            dst_ref=held(c, t),
            send_sem=g_send_sem.at[c, t, way],
            recv_sem=g_recv_sem.at[c, t],
            device_id=to,
            device_id_type=MESH,
        )

    def arrived(c, t):
        shard_copy(c, t, ACROSS).wait_recv()

    def each_own(c, act):
        own = qg_hbm.at[:, :, span(c)]

        @pl.when(z < 3)
        def _():
            act(shard_copy(c, me, UP, own))

        @pl.when(z > 0)
        def _():
            act(shard_copy(c, me, DOWN, own))

        act(shard_copy(c, me, ACROSS, own))

    def each_forward(c, far, act, wait):
        for sign, way in ((-1, UP), (1, DOWN)):
            from_z = z + sign * far
            t = from_z * 2 + x
            there = from_z >= 0 if sign < 0 else from_z < 4
            onward = z < 3 if way == UP else z > 0

            @pl.when(there)
            def _():
                if wait:
                    arrived(c, t)

                @pl.when(onward)
                def _():
                    act(shard_copy(c, t, way))

                if far == 1:

                    @pl.when((c % 2 == 0) | (from_z != zpair))
                    def _():
                        act(shard_copy(c, t, ACROSS))
                else:
                    act(shard_copy(c, t, ACROSS))

    def each_relay(c, act, wait):
        t = z * 2 + 1 - x

        @pl.when(c % 2 == 1)
        def _():
            if wait:
                arrived(c, t)

            @pl.when(z % 2 == 0)
            def _():
                act(shard_copy(c, t, UP))

            @pl.when(z % 2 == 1)
            def _():
                act(shard_copy(c, t, DOWN))

    def start(copy):
        copy.start()

    def sibling_copy(src, dst, sems):
        return pltpu.make_async_remote_copy(
            src_ref=src, dst_ref=dst, send_sem=sems.at[0], recv_sem=sems.at[1], device_id=(sib, me), device_id_type=MESH
        )

    def y_copy(src, dst, sems):
        return pltpu.make_async_remote_copy(
            src_ref=src, dst_ref=dst, send_sem=sems.at[0], recv_sem=sems.at[1], device_id=(ynb, me), device_id_type=MESH
        )

    def part_copy(c):
        return sibling_copy(part_send.at[c], part_recv.at[c], p_sem.at[c])

    def q_copy(c):
        return y_copy(q_send.at[c], q_recv.at[c], q_sem.at[c])

    def s_copy(c):
        return y_copy(s_send.at[c], s_recv.at[c], s_sem.at[c])

    def out_rows(k):
        return pl.ds(pl.multiple_of(k * rows, rows), rows)

    def final_copy(c):
        return sibling_copy(res.at[c], out_hbm.at[out_rows(core), span(c)], f_sem.at[c])

    def out_copy(c):
        return pltpu.make_async_copy(res.at[c], out_hbm.at[out_rows(core), span(c)], o_sem.at[c])

    def dot(a, b):
        return jnp.dot(a, b, preferred_element_type=jnp.float32)

    def dot_nt(a, b):
        return lax.dot_general(a, b, (((1,), (1,)), ((), ())), preferred_element_type=jnp.float32)

    def compute(c, between=None):
        for far in (1, 2, 3):
            other = (z + far) % 4
            arrived(c, other * 2 + 1 - x)

        @pl.when(c % 2 == 0)
        def _():
            arrived(c, z * 2 + 1 - x)

        own_load(c).wait()
        block = gq[c].reshape(micro * mine * 8, cols)
        sums = dot(onehot[...], block)
        high = sums.astype(jnp.bfloat16)
        rest = sums - high.astype(jnp.float32)
        mid = rest.astype(jnp.bfloat16)
        low = (rest - mid.astype(jnp.float32)).astype(jnp.bfloat16)
        w_part = w[:, span(c)]
        terms = dot_nt(jnp.concatenate([high, mid, low], axis=0), w_part)
        slots = bucket.shape[0]
        bucket[...] += terms[0:slots] + terms[slots : 2 * slots] + terms[2 * slots : 3 * slots]
        if between is not None:
            between()
        part_send[c] = dot(emb_t[out_rows(1 - core), :], block)
        part_copy(c).start()
        part_own[c] = dot(emb_t[out_rows(core), :], block)

    def core_sum(c):
        part_copy(c).wait_recv()
        total = part_own[c] + part_recv[c]
        top = jnp.maximum(jnp.max(jnp.abs(total), axis=0, keepdims=True), 1e-30)
        codes = jnp.round(total * (32767.0 / top))
        q_send[c] = codes.astype(jnp.int32).astype(jnp.int16)
        s_send[c] = jnp.broadcast_to(top * (1.0 / 32767.0), s_send.shape[1:])
        q_copy(c).start()
        s_copy(c).start()

    def finish(c):
        q_copy(c).wait_recv()
        s_copy(c).wait_recv()
        here = q_send[c].astype(jnp.int32).astype(jnp.float32) * s_send[c][0:1, :]
        there = q_recv[c].astype(jnp.int32).astype(jnp.float32) * s_recv[c][0:1, :]
        res[c] = jnp.where(y == 0, here, there) + jnp.where(y == 0, there, here)
        final_copy(c).start()
        out_copy(c).start()

    def guarded(c, stage):
        @pl.when((c >= 0) & (c < CHUNKS))
        def _():
            stage(c)

    def forward_stage(far):
        def stage(c):
            each_forward(c, far, start, True)
            if far == 1:
                each_relay(c, start, True)

        return stage

    for c in range(LEAD):
        each_own(c, start)
    for at in (4, 3, 1, 0, 2):
        loads[at].start()
    for c in range(CHUNKS):
        own_load(c).start()

    group = mine * 8
    width = emb_t.shape[0]
    entries = touched.shape[2]
    slice_idx = me * width // SW
    loads[4].wait()
    lists[...] = jnp.full(lists.shape, -1.0, jnp.float32)
    listed = touched[:, 0, :]
    for s in range(1, SLICES):
        listed = jnp.where(slice_idx == s, touched[:, s, :], listed)
    lists[0:8, 0:entries] = listed.astype(jnp.float32)
    lists[8 : 8 + SLICES, 0:entries] = touched[me].astype(jnp.float32)
    columns = lists[...].T
    for s in range(SLICES):
        live_out[:, s, :] = jnp.broadcast_to(columns[0:entries, 8 + s : 9 + s], (entries, live_out.shape[2]))
    loads[3].wait()
    for m in range(micro):
        row = ids[m, pl.ds(slice_idx, 1), :].astype(jnp.float32)
        for o in range(8):
            hit = columns[0:SLOT, o : o + 1] == row
            onehot[o * SLOT : (o + 1) * SLOT, m * group : (m + 1) * group] = jnp.where(hit, 1.0, 0.0).astype(jnp.bfloat16)
    loads[1].wait()
    bucket[...] = dot(onehot[:, 0:group], resid[0]) + dot(onehot[:, group : 2 * group], resid[1])
    loads[0].wait()
    for m in range(micro):
        emb_t[:, m * group : (m + 1) * group] = emb[m].T
    loads[2].wait()

    def sent(copy):
        copy.wait_send()

    def drain(c):
        each_own(c, sent)
        for far in (1, 2, 3):
            each_forward(c, far, sent, False)
        each_relay(c, sent, False)
        part_copy(c).wait_send()
        q_copy(c).wait_send()
        s_copy(c).wait_send()
        final_copy(c).wait()
        out_copy(c).wait()

    def slot(s, carry):
        guarded(s + LEAD - 1, lambda c: each_own(c, start))
        guarded(s - 1, forward_stage(1))
        guarded(s - 2, forward_stage(2))
        guarded(s - 3, forward_stage(3))
        guarded(s - 4, compute)
        guarded(s - 5, core_sum)
        guarded(s - 7, finish)
        guarded(s - 8, drain)
        return carry

    lax.fori_loop(1, CHUNKS + 3, slot, 0)

    def drain_some(low, high):
        def one(c, carry):
            drain(c)
            return carry

        lax.fori_loop(low, high, one, 0)

    half = b_send.shape[1]

    def half_cols(k):
        return pl.ds(pl.multiple_of(k * half, half), half)

    b_copy = sibling_copy(b_send, b_recv, b_sem)

    def send_bucket():
        b_send[...] = bucket[:, half_cols(1 - core)]
        b_copy.start()

    compute(CHUNKS - 1, send_bucket)
    core_sum(CHUNKS - 2)
    b_copy.wait_recv()
    y_send[...] = bucket[:, half_cols(core)] + b_recv[...]
    rows_copy = y_copy(y_send, y_recv, y_sem)
    rows_copy.start()
    core_sum(CHUNKS - 1)
    finish(CHUNKS - 4)
    drain_some(CHUNKS - 5, CHUNKS - 4)
    finish(CHUNKS - 3)
    rows_copy.wait_recv()
    a_send[...] = y_send[...] + y_recv[...]

    def a_copy(step):
        to = (me + step) % 8
        return pltpu.make_async_remote_copy(
            src_ref=a_send.at[pl.ds(pl.multiple_of(to * SLOT, SLOT), SLOT), :],
            dst_ref=a_recv.at[me],
            send_sem=a_send_sem.at[step],
            recv_sem=a_recv_sem.at[me],
            device_id=(dp, to),
            device_id_type=MESH,
        )

    def a_arrived(step):
        origin = (me + 8 - step) % 8
        return pltpu.make_async_remote_copy(
            src_ref=a_send.at[pl.ds(0, SLOT), :],
            dst_ref=a_recv.at[origin],
            send_sem=a_send_sem.at[step],
            recv_sem=a_recv_sem.at[origin],
            device_id=(dp, origin),
            device_id_type=MESH,
        )

    for step in range(1, 8):
        a_copy(step).start()
    a_recv[me] = a_send[pl.ds(pl.multiple_of(me * SLOT, SLOT), SLOT), :]
    finish(CHUNKS - 2)
    drain_some(CHUNKS - 4, CHUNKS - 3)
    for step in range(1, 8):
        a_arrived(step).wait_recv()
    h_copy = sibling_copy(a_recv, sib_recv, h_sem)
    h_copy.start()
    finish(CHUNKS - 1)
    drain_some(CHUNKS - 3, CHUNKS - 1)
    h_copy.wait_recv()
    for t in range(8):
        for k in range(2):
            at = (t % 2) * 2 * half + k * half
            piece = jnp.where(core == k, a_recv[t], sib_recv[t])
            grads_out[:, t // 2, at : at + half] = piece[0:entries]

    h_copy.wait_send()
    b_copy.wait_send()
    rows_copy.wait_send()
    for step in range(1, 8):
        a_copy(step).wait_send()

    drain_some(CHUNKS - 1, CHUNKS)


def fused(
    embedded,
    resid_grad,
    query_grad,
    query_weight,
    ngram_rows,
    touched_rows,
    row_values,
    row_mean,
    row_square,
):
    micro, group, width = embedded.shape
    hidden = query_grad.shape[2]
    tables = touched_rows.shape[0]
    entries = touched_rows.shape[2]
    cols, half, rows = hidden // CHUNKS, width // 2, width // 2
    slots = tables * SLOT
    f32, bf16, i16 = jnp.float32, jnp.bfloat16, jnp.int16
    dma = pltpu.SemaphoreType.DMA
    vmem = pltpu.VMEM
    anywhere = pl.BlockSpec(memory_space=pl.ANY)
    in_hbm = pl.BlockSpec(memory_space=pltpu.HBM)
    in_vmem = pl.BlockSpec(memory_space=pltpu.VMEM)
    operands = (embedded, resid_grad, query_grad, query_weight, ngram_rows.transpose(0, 2, 1), touched_rows)
    operands = [pltpu.with_memory_space_constraint(operand, pltpu.HBM) for operand in operands]
    weight_grad, grads, lists = pl.pallas_call(
        kernel,
        out_shape=(
            jax.ShapeDtypeStruct((width, hidden), f32),
            jax.ShapeDtypeStruct((entries, SLICES, SW), f32),
            jax.ShapeDtypeStruct((entries, SLICES, SW), f32),
        ),
        in_specs=[in_hbm] * 6,
        out_specs=(anywhere, in_vmem, in_vmem),
        scratch_shapes=[
            vmem((micro, SLICES, group), jnp.int32),
            vmem(touched_rows.shape, jnp.int32),
            vmem((128, 128), f32),
            vmem((slots, micro * group), bf16),
            vmem((micro, group, width), bf16),
            vmem((width, micro * group), bf16),
            vmem((micro, group, width), bf16),
            vmem((width, hidden), bf16),
            vmem((CHUNKS, micro, group, cols), bf16),
            vmem((CHUNKS, rows, cols), f32),
            vmem((CHUNKS, rows, cols), f32),
            vmem((CHUNKS, rows, cols), f32),
            vmem((CHUNKS, rows, cols), i16),
            vmem((CHUNKS, rows, cols), i16),
            vmem((CHUNKS, 8, cols), f32),
            vmem((CHUNKS, 8, cols), f32),
            vmem((CHUNKS, rows, cols), f32),
            vmem((slots, width), f32),
            vmem((slots, half), f32),
            vmem((slots, half), f32),
            vmem((slots, half), f32),
            vmem((slots, half), f32),
            vmem((slots, half), f32),
            vmem((tables, SLOT, half), f32),
            vmem((tables, SLOT, half), f32),
            dma((5 + CHUNKS,)),
            dma((CHUNKS, tables, 3)),
            dma((CHUNKS, tables)),
            dma((CHUNKS, 2)),
            dma((CHUNKS, 2)),
            dma((CHUNKS, 2)),
            dma((CHUNKS, 2)),
            dma((CHUNKS,)),
            dma((2,)),
            dma((2,)),
            dma((tables,)),
            dma((tables,)),
            dma((2,)),
        ],
        compiler_params=pltpu.CompilerParams(
            collective_id=0, has_side_effects=True, vmem_limit_bytes=40 * 1024 * 1024
        ),
        cost_estimate=pl.CostEstimate(flops=3 * 10**9, bytes_accessed=2 * 10**7, transcendentals=0),
    )(*operands)

    def turned(rows):
        return rows[0].transpose(1, 0, 2)

    after = adam_rows(grads, turned(row_values), turned(row_mean), turned(row_square), lists >= 0)
    values_next, mean_next, square_next = [rows.transpose(1, 0, 2)[None] for rows in after]
    return (weight_grad, values_next, mean_next, square_next)


def solution(mesh):
    placed = (
        P(None, "dp", "table"),
        P(None, "dp", "table"),
        P(None, ("dp", "table"), None),
        P("table", None),
        P(None, "dp", None),
        P(),
        P("table", None, None, None),
        P("table", None, None, None),
        P("table", None, None, None),
    )
    fits = mesh.shape["dp"] == 4 and mesh.shape["table"] == 8
    return jax.shard_map(
        fused if fits else local,
        mesh=mesh,
        in_specs=placed,
        out_specs=(
            P("table", None),
            P("table", None, None, None),
            P("table", None, None, None),
            P("table", None, None, None),
        ),
        check_vma=False,
    )
```

```python
import functools

import jax
import jax.numpy as jnp
from jax import lax
from jax.experimental import pallas as pl
from jax.experimental.pallas import tpu as pltpu
from jax.sharding import PartitionSpec as P

SLICES = 4
SW = 1024


beta_one = 0.9
beta_two = 0.95
learn_rate = 0.01
adam_eps = 1e-08
adam_step = 10


def adam_rows(grads, values, mean, square, live):
    corr_one = 1.0 - beta_one**adam_step
    corr_two = 1.0 - beta_two**adam_step
    mean_next = beta_one * mean + (1.0 - beta_one) * grads
    square_next = beta_two * square + (1.0 - beta_two) * grads * grads
    update = learn_rate * (mean_next / corr_one) / (jnp.sqrt(square_next / corr_two) + adam_eps)
    values_next = values - update
    return (
        jnp.where(live, values_next, values),
        jnp.where(live, mean_next, mean),
        jnp.where(live, square_next, square),
    )


def make_step(emb_part, weight_part, carry, piece):
    back_part, wgrad = carry
    back = jnp.einsum("mrh,ph->mrp", piece, weight_part, preferred_element_type=jnp.float32)
    back_part = back
    wgrad = wgrad + jnp.einsum("mrp,mrh->ph", emb_part, piece, preferred_element_type=jnp.float32)
    return (back_part, wgrad)


def local(
    embedded,
    resid_grad,
    query_grad,
    query_weight,
    ngram_rows,
    touched_rows,
    row_values,
    row_mean,
    row_square,
):
    micro_count, group_tokens, width_part = embedded.shape
    hidden = query_grad.shape[2]
    tables = lax.axis_size("table")
    table_idx = lax.axis_index("table")
    zero_grad = jnp.zeros((width_part, hidden), jnp.float32)
    wgrad = zero_grad
    backs = []
    for micro in range(micro_count):
        start_back = jnp.zeros((1, group_tokens, width_part), jnp.float32)
        back_one, wgrad = make_step(
            embedded[micro : micro + 1],
            query_weight,
            (start_back, wgrad),
            lax.all_gather(query_grad[micro : micro + 1], "table", axis=1, tiled=True),
        )
        backs.append(back_one)
    back_all = jnp.concatenate(backs, axis=0)
    emb_grad = resid_grad.astype(jnp.float32) + back_all
    weight_grad = lax.psum(wgrad, "dp")
    slice_idx = table_idx * width_part // SW
    ids = lax.dynamic_index_in_dim(ngram_rows, slice_idx, 2, False)
    listed = lax.dynamic_index_in_dim(touched_rows, slice_idx, 1, False)
    entries = listed.shape[1]
    flat_list = listed.reshape(tables * entries)
    onehot = (ids[:, :, None] == flat_list[None, None, :]).astype(jnp.float32)
    buckets = jnp.einsum(
        "mtk,mtp->kp",
        onehot,
        emb_grad,
        precision=lax.Precision.HIGHEST,
        preferred_element_type=jnp.float32,
    )
    buckets = buckets.reshape(tables, entries, width_part)
    arrived = lax.all_to_all(buckets, "table", split_axis=0, concat_axis=0, tiled=True)
    per_slice = tables // SLICES
    local_grad = (
        arrived.reshape(SLICES, per_slice, entries, width_part)
        .transpose(0, 2, 1, 3)
        .reshape(SLICES, entries, per_slice * width_part)
    )
    mine = lax.dynamic_index_in_dim(touched_rows, table_idx, 0, False)
    live = (mine >= 0)[..., None]
    values = row_values[0]
    mean = row_mean[0]
    square = row_square[0]
    grads = lax.psum(local_grad, "dp")
    values_next, mean_next, square_next = adam_rows(grads, values, mean, square, live)
    return (weight_grad, values_next[None], mean_next[None], square_next[None])


LEAD = 6
CHUNKS = 16
SLOT = 16
MESH = pl.DeviceIdType.MESH
UP, DOWN, ACROSS = 0, 1, 2


def kernel(
    emb_hbm,
    resid_hbm,
    qg_hbm,
    w_hbm,
    ids_hbm,
    touched_hbm,
    out_hbm,
    grads_out,
    live_out,
    ids,
    touched,
    lists,
    onehot,
    emb,
    emb_t,
    resid,
    w,
    gq,
    part_own,
    part_send,
    part_recv,
    q_send,
    q_recv,
    s_send,
    s_recv,
    res,
    bucket,
    b_send,
    b_recv,
    y_send,
    y_recv,
    a_send,
    a_recv,
    sib_recv,
    load_sem,
    g_send_sem,
    g_recv_sem,
    p_sem,
    q_sem,
    s_sem,
    f_sem,
    o_sem,
    b_sem,
    y_sem,
    a_send_sem,
    a_recv_sem,
    h_sem,
):
    dp, me = lax.axis_index("dp"), lax.axis_index("table")
    y, core = dp // 2, dp % 2
    z, x = me // 2, me % 2
    sib = dp + 1 - 2 * core
    ynb = (1 - y) * 2 + core
    zpair = z + 1 - 2 * (z % 2)
    micro, mine, hidden = qg_hbm.shape
    cols = hidden // CHUNKS
    rows = emb_t.shape[0] // 2

    barrier = pltpu.get_barrier_semaphore()
    for step in range(1, 8):
        pl.semaphore_signal(barrier, inc=1, device_id=(dp, (me + step) % 8), device_id_type=MESH)
    pl.semaphore_signal(barrier, inc=1, device_id=(sib, me), device_id_type=MESH)
    pl.semaphore_signal(barrier, inc=1, device_id=(ynb, me), device_id_type=MESH)

    loads = [
        pltpu.make_async_copy(emb_hbm, emb, load_sem.at[0]),
        pltpu.make_async_copy(resid_hbm, resid, load_sem.at[1]),
        pltpu.make_async_copy(w_hbm, w, load_sem.at[2]),
        pltpu.make_async_copy(ids_hbm, ids, load_sem.at[3]),
        pltpu.make_async_copy(touched_hbm, touched, load_sem.at[4]),
    ]

    def span(c):
        return pl.ds(pl.multiple_of(c * cols, cols), cols)

    def tokens(t):
        return pl.ds(pl.multiple_of(t * mine, mine), mine)

    def held(c, t):
        return gq.at[c, :, tokens(t), :]

    def own_load(c):
        return pltpu.make_async_copy(qg_hbm.at[:, :, span(c)], held(c, me), load_sem.at[5 + c])

    pl.semaphore_wait(barrier, 9)

    def shard_copy(c, t, way, source=None):
        to_z = z + 1 if way == UP else z - 1
        to = (dp, to_z * 2 + x) if way != ACROSS else (dp, z * 2 + 1 - x)
        return pltpu.make_async_remote_copy(
            src_ref=held(c, t) if source is None else source,
            dst_ref=held(c, t),
            send_sem=g_send_sem.at[c, t, way],
            recv_sem=g_recv_sem.at[c, t],
            device_id=to,
            device_id_type=MESH,
        )

    def arrived(c, t):
        shard_copy(c, t, ACROSS).wait_recv()

    def each_own(c, act):
        own = qg_hbm.at[:, :, span(c)]

        @pl.when(z < 3)
        def _():
            act(shard_copy(c, me, UP, own))

        @pl.when(z > 0)
        def _():
            act(shard_copy(c, me, DOWN, own))

        act(shard_copy(c, me, ACROSS, own))

    def each_forward(c, far, act, wait):
        for sign, way in ((-1, UP), (1, DOWN)):
            from_z = z + sign * far
            t = from_z * 2 + x
            there = from_z >= 0 if sign < 0 else from_z < 4
            onward = z < 3 if way == UP else z > 0

            @pl.when(there)
            def _():
                if wait:
                    arrived(c, t)

                @pl.when(onward)
                def _():
                    act(shard_copy(c, t, way))

                if far == 1:

                    @pl.when((c % 2 == 0) | (from_z != zpair))
                    def _():
                        act(shard_copy(c, t, ACROSS))
                else:
                    act(shard_copy(c, t, ACROSS))

    def each_relay(c, act, wait):
        t = z * 2 + 1 - x

        @pl.when(c % 2 == 1)
        def _():
            if wait:
                arrived(c, t)

            @pl.when(z % 2 == 0)
            def _():
                act(shard_copy(c, t, UP))

            @pl.when(z % 2 == 1)
            def _():
                act(shard_copy(c, t, DOWN))

    def start(copy):
        copy.start()

    def sibling_copy(src, dst, sems):
        return pltpu.make_async_remote_copy(
            src_ref=src, dst_ref=dst, send_sem=sems.at[0], recv_sem=sems.at[1], device_id=(sib, me), device_id_type=MESH
        )

    def y_copy(src, dst, sems):
        return pltpu.make_async_remote_copy(
            src_ref=src, dst_ref=dst, send_sem=sems.at[0], recv_sem=sems.at[1], device_id=(ynb, me), device_id_type=MESH
        )

    def part_copy(c):
        return sibling_copy(part_send.at[c], part_recv.at[c], p_sem.at[c])

    def q_copy(c):
        return y_copy(q_send.at[c], q_recv.at[c], q_sem.at[c])

    def s_copy(c):
        return y_copy(s_send.at[c], s_recv.at[c], s_sem.at[c])

    def out_rows(k):
        return pl.ds(pl.multiple_of(k * rows, rows), rows)

    def final_copy(c):
        return sibling_copy(res.at[c], out_hbm.at[out_rows(core), span(c)], f_sem.at[c])

    def out_copy(c):
        return pltpu.make_async_copy(res.at[c], out_hbm.at[out_rows(core), span(c)], o_sem.at[c])

    def dot(a, b):
        return jnp.dot(a, b, preferred_element_type=jnp.float32)

    def dot_nt(a, b):
        return lax.dot_general(a, b, (((1,), (1,)), ((), ())), preferred_element_type=jnp.float32)

    def compute(c, between=None):
        for far in (1, 2, 3):
            other = (z + far) % 4
            arrived(c, other * 2 + 1 - x)

        @pl.when(c % 2 == 0)
        def _():
            arrived(c, z * 2 + 1 - x)

        own_load(c).wait()
        block = gq[c].reshape(micro * mine * 8, cols)
        sums = dot(onehot[...], block)
        high = sums.astype(jnp.bfloat16)
        rest = sums - high.astype(jnp.float32)
        mid = rest.astype(jnp.bfloat16)
        low = (rest - mid.astype(jnp.float32)).astype(jnp.bfloat16)
        w_part = w[:, span(c)]
        terms = dot_nt(jnp.concatenate([high, mid, low], axis=0), w_part)
        slots = bucket.shape[0]
        bucket[...] += terms[0:slots] + terms[slots : 2 * slots] + terms[2 * slots : 3 * slots]
        if between is not None:
            between()
        part_send[c] = dot(emb_t[out_rows(1 - core), :], block)
        part_copy(c).start()
        part_own[c] = dot(emb_t[out_rows(core), :], block)

    def core_sum(c):
        part_copy(c).wait_recv()
        total = part_own[c] + part_recv[c]
        top = jnp.maximum(jnp.max(jnp.abs(total), axis=0, keepdims=True), 1e-30)
        codes = jnp.round(total * (32767.0 / top))
        q_send[c] = codes.astype(jnp.int32).astype(jnp.int16)
        s_send[c] = jnp.broadcast_to(top * (1.0 / 32767.0), s_send.shape[1:])
        q_copy(c).start()
        s_copy(c).start()

    def finish(c):
        q_copy(c).wait_recv()
        s_copy(c).wait_recv()
        here = q_send[c].astype(jnp.int32).astype(jnp.float32) * s_send[c][0:1, :]
        there = q_recv[c].astype(jnp.int32).astype(jnp.float32) * s_recv[c][0:1, :]
        res[c] = jnp.where(y == 0, here, there) + jnp.where(y == 0, there, here)
        final_copy(c).start()
        out_copy(c).start()

    def guarded(c, stage):
        @pl.when((c >= 0) & (c < CHUNKS))
        def _():
            stage(c)

    def forward_stage(far):
        def stage(c):
            each_forward(c, far, start, True)
            if far == 1:
                each_relay(c, start, True)

        return stage

    for c in range(LEAD):
        each_own(c, start)
    for at in (4, 3, 1, 0, 2):
        loads[at].start()
    for c in range(CHUNKS):
        own_load(c).start()

    group = mine * 8
    width = emb_t.shape[0]
    entries = touched.shape[2]
    slice_idx = me * width // SW
    loads[4].wait()
    lists[...] = jnp.full(lists.shape, -1.0, jnp.float32)
    listed = touched[:, 0, :]
    for s in range(1, SLICES):
        listed = jnp.where(slice_idx == s, touched[:, s, :], listed)
    lists[0:8, 0:entries] = listed.astype(jnp.float32)
    lists[8 : 8 + SLICES, 0:entries] = touched[me].astype(jnp.float32)
    columns = lists[...].T
    for s in range(SLICES):
        live_out[:, s, :] = jnp.broadcast_to(columns[0:entries, 8 + s : 9 + s], (entries, live_out.shape[2]))
    loads[3].wait()
    for m in range(micro):
        row = ids[m, pl.ds(slice_idx, 1), :].astype(jnp.float32)
        for o in range(8):
            hit = columns[0:SLOT, o : o + 1] == row
            onehot[o * SLOT : (o + 1) * SLOT, m * group : (m + 1) * group] = jnp.where(hit, 1.0, 0.0).astype(jnp.bfloat16)
    loads[1].wait()
    bucket[...] = dot(onehot[:, 0:group], resid[0]) + dot(onehot[:, group : 2 * group], resid[1])
    loads[0].wait()
    for m in range(micro):
        emb_t[:, m * group : (m + 1) * group] = emb[m].T
    loads[2].wait()

    def sent(copy):
        copy.wait_send()

    def drain(c):
        each_own(c, sent)
        for far in (1, 2, 3):
            each_forward(c, far, sent, False)
        each_relay(c, sent, False)
        part_copy(c).wait_send()
        q_copy(c).wait_send()
        s_copy(c).wait_send()
        final_copy(c).wait()
        out_copy(c).wait()

    def slot(s, carry):
        guarded(s + LEAD - 1, lambda c: each_own(c, start))
        guarded(s - 1, forward_stage(1))
        guarded(s - 2, forward_stage(2))
        guarded(s - 3, forward_stage(3))
        guarded(s - 4, compute)
        guarded(s - 5, core_sum)
        guarded(s - 7, finish)
        guarded(s - 8, drain)
        return carry

    lax.fori_loop(1, CHUNKS + 3, slot, 0)

    def drain_some(low, high):
        def one(c, carry):
            drain(c)
            return carry

        lax.fori_loop(low, high, one, 0)

    half = b_send.shape[1]

    def half_cols(k):
        return pl.ds(pl.multiple_of(k * half, half), half)

    b_copy = sibling_copy(b_send, b_recv, b_sem)

    def send_bucket():
        b_send[...] = bucket[:, half_cols(1 - core)]
        b_copy.start()

    compute(CHUNKS - 1, send_bucket)
    core_sum(CHUNKS - 2)
    b_copy.wait_recv()
    y_send[...] = bucket[:, half_cols(core)] + b_recv[...]
    rows_copy = y_copy(y_send, y_recv, y_sem)
    rows_copy.start()
    core_sum(CHUNKS - 1)
    finish(CHUNKS - 4)
    drain_some(CHUNKS - 5, CHUNKS - 4)
    finish(CHUNKS - 3)
    rows_copy.wait_recv()
    a_send[...] = y_send[...] + y_recv[...]

    def a_copy(step):
        to = (me + step) % 8
        return pltpu.make_async_remote_copy(
            src_ref=a_send.at[pl.ds(pl.multiple_of(to * SLOT, SLOT), SLOT), :],
            dst_ref=a_recv.at[me],
            send_sem=a_send_sem.at[step],
            recv_sem=a_recv_sem.at[me],
            device_id=(dp, to),
            device_id_type=MESH,
        )

    def a_arrived(step):
        origin = (me + 8 - step) % 8
        return pltpu.make_async_remote_copy(
            src_ref=a_send.at[pl.ds(0, SLOT), :],
            dst_ref=a_recv.at[origin],
            send_sem=a_send_sem.at[step],
            recv_sem=a_recv_sem.at[origin],
            device_id=(dp, origin),
            device_id_type=MESH,
        )

    for step in range(1, 8):
        a_copy(step).start()
    a_recv[me] = a_send[pl.ds(pl.multiple_of(me * SLOT, SLOT), SLOT), :]
    finish(CHUNKS - 2)
    drain_some(CHUNKS - 4, CHUNKS - 3)
    for step in range(1, 8):
        a_arrived(step).wait_recv()
    h_copy = sibling_copy(a_recv, sib_recv, h_sem)
    h_copy.start()
    finish(CHUNKS - 1)
    drain_some(CHUNKS - 3, CHUNKS - 1)
    h_copy.wait_recv()
    for t in range(8):
        for k in range(2):
            at = (t % 2) * 2 * half + k * half
            piece = jnp.where(core == k, a_recv[t], sib_recv[t])
            grads_out[:, t // 2, at : at + half] = piece[0:entries]

    h_copy.wait_send()
    b_copy.wait_send()
    rows_copy.wait_send()
    for step in range(1, 8):
        a_copy(step).wait_send()

    drain_some(CHUNKS - 1, CHUNKS)


def fused(
    embedded,
    resid_grad,
    query_grad,
    query_weight,
    ngram_rows,
    touched_rows,
    row_values,
    row_mean,
    row_square,
):
    micro, group, width = embedded.shape
    hidden = query_grad.shape[2]
    tables = touched_rows.shape[0]
    entries = touched_rows.shape[2]
    cols, half, rows = hidden // CHUNKS, width // 2, width // 2
    slots = tables * SLOT
    f32, bf16, i16 = jnp.float32, jnp.bfloat16, jnp.int16
    dma = pltpu.SemaphoreType.DMA
    vmem = pltpu.VMEM
    anywhere = pl.BlockSpec(memory_space=pl.ANY)
    in_hbm = pl.BlockSpec(memory_space=pltpu.HBM)
    in_vmem = pl.BlockSpec(memory_space=pltpu.VMEM)
    operands = (embedded, resid_grad, query_grad, query_weight, ngram_rows.transpose(0, 2, 1), touched_rows)
    operands = [pltpu.with_memory_space_constraint(operand, pltpu.HBM) for operand in operands]
    weight_grad, grads, lists = pl.pallas_call(
        kernel,
        out_shape=(
            jax.ShapeDtypeStruct((width, hidden), f32),
            jax.ShapeDtypeStruct((entries, SLICES, SW), f32),
            jax.ShapeDtypeStruct((entries, SLICES, SW), f32),
        ),
        in_specs=[in_hbm] * 6,
        out_specs=(anywhere, in_vmem, in_vmem),
        scratch_shapes=[
            vmem((micro, SLICES, group), jnp.int32),
            vmem(touched_rows.shape, jnp.int32),
            vmem((128, 128), f32),
            vmem((slots, micro * group), bf16),
            vmem((micro, group, width), bf16),
            vmem((width, micro * group), bf16),
            vmem((micro, group, width), bf16),
            vmem((width, hidden), bf16),
            vmem((CHUNKS, micro, group, cols), bf16),
            vmem((CHUNKS, rows, cols), f32),
            vmem((CHUNKS, rows, cols), f32),
            vmem((CHUNKS, rows, cols), f32),
            vmem((CHUNKS, rows, cols), i16),
            vmem((CHUNKS, rows, cols), i16),
            vmem((CHUNKS, 8, cols), f32),
            vmem((CHUNKS, 8, cols), f32),
            vmem((CHUNKS, rows, cols), f32),
            vmem((slots, width), f32),
            vmem((slots, half), f32),
            vmem((slots, half), f32),
            vmem((slots, half), f32),
            vmem((slots, half), f32),
            vmem((slots, half), f32),
            vmem((tables, SLOT, half), f32),
            vmem((tables, SLOT, half), f32),
            dma((5 + CHUNKS,)),
            dma((CHUNKS, tables, 3)),
            dma((CHUNKS, tables)),
            dma((CHUNKS, 2)),
            dma((CHUNKS, 2)),
            dma((CHUNKS, 2)),
            dma((CHUNKS, 2)),
            dma((CHUNKS,)),
            dma((2,)),
            dma((2,)),
            dma((tables,)),
            dma((tables,)),
            dma((2,)),
        ],
        compiler_params=pltpu.CompilerParams(
            collective_id=0, has_side_effects=True, vmem_limit_bytes=40 * 1024 * 1024
        ),
        cost_estimate=pl.CostEstimate(flops=3 * 10**9, bytes_accessed=2 * 10**7, transcendentals=0),
    )(*operands)

    def turned(rows):
        return rows[0].transpose(1, 0, 2)

    after = adam_rows(grads, turned(row_values), turned(row_mean), turned(row_square), lists >= 0)
    values_next, mean_next, square_next = [rows.transpose(1, 0, 2)[None] for rows in after]
    return (weight_grad, values_next, mean_next, square_next)


def solution(mesh):
    placed = (
        P(None, "dp", "table"),
        P(None, "dp", "table"),
        P(None, ("dp", "table"), None),
        P("table", None),
        P(None, "dp", None),
        P(),
        P("table", None, None, None),
        P("table", None, None, None),
        P("table", None, None, None),
    )
    fits = mesh.shape["dp"] == 4 and mesh.shape["table"] == 8
    return jax.shard_map(
        fused if fits else local,
        mesh=mesh,
        in_specs=placed,
        out_specs=(
            P("table", None),
            P("table", None, None, None),
            P("table", None, None, None),
            P("table", None, None, None),
        ),
        check_vma=False,
    )
```

```python
import functools

import jax
import jax.numpy as jnp
from jax import lax
from jax.experimental import pallas as pl
from jax.experimental.pallas import tpu as pltpu
from jax.sharding import PartitionSpec as P

SLICES = 4
SW = 1024


beta_one = 0.9
beta_two = 0.95
learn_rate = 0.01
adam_eps = 1e-08
adam_step = 10


def adam_rows(grads, values, mean, square, live):
    corr_one = 1.0 - beta_one**adam_step
    corr_two = 1.0 - beta_two**adam_step
    mean_next = beta_one * mean + (1.0 - beta_one) * grads
    square_next = beta_two * square + (1.0 - beta_two) * grads * grads
    update = learn_rate * (mean_next / corr_one) / (jnp.sqrt(square_next / corr_two) + adam_eps)
    values_next = values - update
    return (
        jnp.where(live, values_next, values),
        jnp.where(live, mean_next, mean),
        jnp.where(live, square_next, square),
    )


def make_step(emb_part, weight_part, carry, piece):
    back_part, wgrad = carry
    back = jnp.einsum("mrh,ph->mrp", piece, weight_part, preferred_element_type=jnp.float32)
    back_part = back
    wgrad = wgrad + jnp.einsum("mrp,mrh->ph", emb_part, piece, preferred_element_type=jnp.float32)
    return (back_part, wgrad)


def local(
    embedded,
    resid_grad,
    query_grad,
    query_weight,
    ngram_rows,
    touched_rows,
    row_values,
    row_mean,
    row_square,
):
    micro_count, group_tokens, width_part = embedded.shape
    hidden = query_grad.shape[2]
    tables = lax.axis_size("table")
    table_idx = lax.axis_index("table")
    zero_grad = jnp.zeros((width_part, hidden), jnp.float32)
    wgrad = zero_grad
    backs = []
    for micro in range(micro_count):
        start_back = jnp.zeros((1, group_tokens, width_part), jnp.float32)
        back_one, wgrad = make_step(
            embedded[micro : micro + 1],
            query_weight,
            (start_back, wgrad),
            lax.all_gather(query_grad[micro : micro + 1], "table", axis=1, tiled=True),
        )
        backs.append(back_one)
    back_all = jnp.concatenate(backs, axis=0)
    emb_grad = resid_grad.astype(jnp.float32) + back_all
    weight_grad = lax.psum(wgrad, "dp")
    slice_idx = table_idx * width_part // SW
    ids = lax.dynamic_index_in_dim(ngram_rows, slice_idx, 2, False)
    listed = lax.dynamic_index_in_dim(touched_rows, slice_idx, 1, False)
    entries = listed.shape[1]
    flat_list = listed.reshape(tables * entries)
    onehot = (ids[:, :, None] == flat_list[None, None, :]).astype(jnp.float32)
    buckets = jnp.einsum(
        "mtk,mtp->kp",
        onehot,
        emb_grad,
        precision=lax.Precision.HIGHEST,
        preferred_element_type=jnp.float32,
    )
    buckets = buckets.reshape(tables, entries, width_part)
    arrived = lax.all_to_all(buckets, "table", split_axis=0, concat_axis=0, tiled=True)
    per_slice = tables // SLICES
    local_grad = (
        arrived.reshape(SLICES, per_slice, entries, width_part)
        .transpose(0, 2, 1, 3)
        .reshape(SLICES, entries, per_slice * width_part)
    )
    mine = lax.dynamic_index_in_dim(touched_rows, table_idx, 0, False)
    live = (mine >= 0)[..., None]
    values = row_values[0]
    mean = row_mean[0]
    square = row_square[0]
    grads = lax.psum(local_grad, "dp")
    values_next, mean_next, square_next = adam_rows(grads, values, mean, square, live)
    return (weight_grad, values_next[None], mean_next[None], square_next[None])


LEAD = 3
CHUNKS = 8
SLOT = 16
MESH = pl.DeviceIdType.MESH
UP, DOWN, ACROSS = 0, 1, 2


def kernel(
    emb_hbm,
    resid_hbm,
    qg_hbm,
    w_hbm,
    ids_hbm,
    touched_hbm,
    out_hbm,
    grads_out,
    live_out,
    ids,
    touched,
    lists,
    emb,
    left,
    resid,
    w,
    gq,
    prod,
    part_recv,
    q_send,
    q_recv,
    s_send,
    s_recv,
    res,
    bucket,
    b_send,
    b_recv,
    y_send,
    y_recv,
    a_send,
    a_recv,
    sib_recv,
    load_sem,
    g_send_sem,
    g_recv_sem,
    p_sem,
    q_sem,
    s_sem,
    f_sem,
    o_sem,
    b_sem,
    y_sem,
    a_send_sem,
    a_recv_sem,
    h_sem,
):
    dp, me = lax.axis_index("dp"), lax.axis_index("table")
    y, core = dp // 2, dp % 2
    z, x = me // 2, me % 2
    sib = dp + 1 - 2 * core
    ynb = (1 - y) * 2 + core
    zpair = z + 1 - 2 * (z % 2)
    micro, mine, hidden = qg_hbm.shape
    cols = hidden // CHUNKS
    width = emb.shape[2]
    rows = width // 2

    barrier = pltpu.get_barrier_semaphore()
    for step in range(1, 8):
        pl.semaphore_signal(barrier, inc=1, device_id=(dp, (me + step) % 8), device_id_type=MESH)
    pl.semaphore_signal(barrier, inc=1, device_id=(sib, me), device_id_type=MESH)
    pl.semaphore_signal(barrier, inc=1, device_id=(ynb, me), device_id_type=MESH)

    loads = [
        pltpu.make_async_copy(emb_hbm, emb, load_sem.at[0]),
        pltpu.make_async_copy(resid_hbm, resid, load_sem.at[1]),
        pltpu.make_async_copy(w_hbm, w, load_sem.at[2]),
        pltpu.make_async_copy(ids_hbm, ids, load_sem.at[3]),
        pltpu.make_async_copy(touched_hbm, touched, load_sem.at[4]),
    ]

    def span(c):
        return pl.ds(pl.multiple_of(c * cols, cols), cols)

    def tokens(t):
        return pl.ds(pl.multiple_of(t * mine, mine), mine)

    def held(c, t):
        return gq.at[c, :, tokens(t), :]

    def own_load(c):
        return pltpu.make_async_copy(qg_hbm.at[:, :, span(c)], held(c, me), load_sem.at[5 + c])

    pl.semaphore_wait(barrier, 9)

    def shard_copy(c, t, way, source=None):
        to_z = z + 1 if way == UP else z - 1
        to = (dp, to_z * 2 + x) if way != ACROSS else (dp, z * 2 + 1 - x)
        return pltpu.make_async_remote_copy(
            src_ref=held(c, t) if source is None else source,
            dst_ref=held(c, t),
            send_sem=g_send_sem.at[c, t, way],
            recv_sem=g_recv_sem.at[c, t],
            device_id=to,
            device_id_type=MESH,
        )

    def arrived(c, t):
        shard_copy(c, t, ACROSS).wait_recv()

    def each_own(c, act):
        own = qg_hbm.at[:, :, span(c)]

        @pl.when(z < 3)
        def _():
            act(shard_copy(c, me, UP, own))

        @pl.when(z > 0)
        def _():
            act(shard_copy(c, me, DOWN, own))

        act(shard_copy(c, me, ACROSS, own))

    def each_forward(c, far, act, wait):
        for sign, way in ((-1, UP), (1, DOWN)):
            from_z = z + sign * far
            t = from_z * 2 + x
            there = from_z >= 0 if sign < 0 else from_z < 4
            onward = z < 3 if way == UP else z > 0

            @pl.when(there)
            def _():
                if wait:
                    arrived(c, t)

                @pl.when(onward)
                def _():
                    act(shard_copy(c, t, way))

                if far == 1:

                    @pl.when((c % 2 == 0) | (from_z != zpair))
                    def _():
                        act(shard_copy(c, t, ACROSS))
                else:
                    act(shard_copy(c, t, ACROSS))

    def each_relay(c, act, wait):
        t = z * 2 + 1 - x

        @pl.when(c % 2 == 1)
        def _():
            if wait:
                arrived(c, t)

            @pl.when(z % 2 == 0)
            def _():
                act(shard_copy(c, t, UP))

            @pl.when(z % 2 == 1)
            def _():
                act(shard_copy(c, t, DOWN))

    def start(copy):
        copy.start()

    def sibling_copy(src, dst, sems):
        return pltpu.make_async_remote_copy(
            src_ref=src, dst_ref=dst, send_sem=sems.at[0], recv_sem=sems.at[1], device_id=(sib, me), device_id_type=MESH
        )

    def y_copy(src, dst, sems):
        return pltpu.make_async_remote_copy(
            src_ref=src, dst_ref=dst, send_sem=sems.at[0], recv_sem=sems.at[1], device_id=(ynb, me), device_id_type=MESH
        )

    def part_copy(c):
        return sibling_copy(prod.at[c, 0:rows], part_recv.at[c], p_sem.at[c])

    def q_copy(c):
        return y_copy(q_send.at[c], q_recv.at[c], q_sem.at[c])

    def s_copy(c):
        return y_copy(s_send.at[c], s_recv.at[c], s_sem.at[c])

    def out_rows(k):
        return pl.ds(pl.multiple_of(k * rows, rows), rows)

    def final_copy(c):
        return sibling_copy(res.at[c], out_hbm.at[out_rows(core), span(c)], f_sem.at[c])

    def out_copy(c):
        return pltpu.make_async_copy(res.at[c], out_hbm.at[out_rows(core), span(c)], o_sem.at[c])

    def dot(a, b):
        return jnp.dot(a, b, preferred_element_type=jnp.float32)

    def dot_nt(a, b):
        return lax.dot_general(a, b, (((1,), (1,)), ((), ())), preferred_element_type=jnp.float32)

    def compute(c):
        for far in (1, 2, 3):
            other = (z + far) % 4
            arrived(c, other * 2 + 1 - x)

        @pl.when(c % 2 == 0)
        def _():
            arrived(c, z * 2 + 1 - x)

        own_load(c).wait()
        block = gq[c].reshape(micro * mine * 8, cols)
        prod[c] = dot(left[...], block)
        part_copy(c).start()
        sums = prod[c, width:, :]
        high = sums.astype(jnp.bfloat16)
        low = (sums - high.astype(jnp.float32)).astype(jnp.bfloat16)
        terms = dot_nt(jnp.concatenate([high, low], axis=0), w[:, span(c)])
        slots = bucket.shape[0]
        bucket[...] += terms[0:slots] + terms[slots : 2 * slots]

    def core_sum(c):
        part_copy(c).wait_recv()
        total = prod[c, rows:width, :] + part_recv[c]
        top = jnp.maximum(jnp.max(jnp.abs(total), axis=0, keepdims=True), 1e-30)
        codes = jnp.round(total * (32767.0 / top))
        q_send[c] = codes.astype(jnp.int32).astype(jnp.int16)
        s_send[c] = jnp.broadcast_to(top * (1.0 / 32767.0), s_send.shape[1:])
        q_copy(c).start()
        s_copy(c).start()

    def finish(c):
        q_copy(c).wait_recv()
        s_copy(c).wait_recv()
        here = q_send[c].astype(jnp.int32).astype(jnp.float32) * s_send[c][0:1, :]
        there = q_recv[c].astype(jnp.int32).astype(jnp.float32) * s_recv[c][0:1, :]
        res[c] = jnp.where(y == 0, here, there) + jnp.where(y == 0, there, here)
        final_copy(c).start()
        out_copy(c).start()

    def guarded(c, stage):
        @pl.when((c >= 0) & (c < CHUNKS))
        def _():
            stage(c)

    def forward_stage(far):
        def stage(c):
            each_forward(c, far, start, True)
            if far == 1:
                each_relay(c, start, True)

        return stage

    for c in range(LEAD):
        each_own(c, start)
    for at in (4, 3, 1, 0, 2):
        loads[at].start()
    for c in range(CHUNKS):
        own_load(c).start()

    group = mine * 8
    entries = touched.shape[2]
    slice_idx = me * width // SW
    loads[4].wait()
    lists[...] = jnp.full(lists.shape, -1.0, jnp.float32)
    listed = touched[:, 0, :]
    for s in range(1, SLICES):
        listed = jnp.where(slice_idx == s, touched[:, s, :], listed)
    lists[0:8, 0:entries] = listed.astype(jnp.float32)
    lists[8 : 8 + SLICES, 0:entries] = touched[me].astype(jnp.float32)
    columns = lists[...].T
    for s in range(SLICES):
        live_out[:, s, :] = jnp.broadcast_to(columns[0:entries, 8 + s : 9 + s], (entries, live_out.shape[2]))
    loads[3].wait()
    for m in range(micro):
        row = ids[m, pl.ds(slice_idx, 1), :].astype(jnp.float32)
        for o in range(8):
            hit = columns[0:SLOT, o : o + 1] == row
            left[width + o * SLOT : width + (o + 1) * SLOT, m * group : (m + 1) * group] = jnp.where(hit, 1.0, 0.0).astype(jnp.bfloat16)
    loads[1].wait()
    bucket[...] = dot(left[width:, 0:group], resid[0]) + dot(left[width:, group : 2 * group], resid[1])
    loads[0].wait()
    for m in range(micro):
        for k in range(2):
            first = rows * (1 - core) if k == 0 else rows * core
            block = emb[m, :, k * rows : (k + 1) * rows].T
            left[pl.ds(pl.multiple_of(first, rows), rows), m * group : (m + 1) * group] = block
    loads[2].wait()

    def sent(copy):
        copy.wait_send()

    def drain(c):
        each_own(c, sent)
        for far in (1, 2, 3):
            each_forward(c, far, sent, False)
        each_relay(c, sent, False)
        part_copy(c).wait_send()
        q_copy(c).wait_send()
        s_copy(c).wait_send()
        final_copy(c).wait()
        out_copy(c).wait()

    def slot(s, carry):
        guarded(s + LEAD - 1, lambda c: each_own(c, start))
        guarded(s - 1, forward_stage(1))
        guarded(s - 2, forward_stage(2))
        guarded(s - 3, forward_stage(3))
        guarded(s - 4, compute)
        guarded(s - 5, core_sum)
        guarded(s - 7, finish)
        guarded(s - 8, drain)
        return carry

    lax.fori_loop(1, CHUNKS + 3, slot, 0)

    def drain_some(low, high):
        def one(c, carry):
            drain(c)
            return carry

        lax.fori_loop(low, high, one, 0)

    half = b_send.shape[1]

    def half_cols(k):
        return pl.ds(pl.multiple_of(k * half, half), half)

    b_copy = sibling_copy(b_send, b_recv, b_sem)
    compute(CHUNKS - 1)
    b_send[...] = bucket[:, half_cols(1 - core)]
    b_copy.start()
    core_sum(CHUNKS - 2)
    b_copy.wait_recv()
    y_send[...] = bucket[:, half_cols(core)] + b_recv[...]
    rows_copy = y_copy(y_send, y_recv, y_sem)
    rows_copy.start()
    core_sum(CHUNKS - 1)
    finish(CHUNKS - 4)
    drain_some(CHUNKS - 5, CHUNKS - 4)
    finish(CHUNKS - 3)
    rows_copy.wait_recv()
    a_send[...] = y_send[...] + y_recv[...]

    def a_copy(step):
        to = (me + step) % 8
        return pltpu.make_async_remote_copy(
            src_ref=a_send.at[pl.ds(pl.multiple_of(to * SLOT, SLOT), SLOT), :],
            dst_ref=a_recv.at[me],
            send_sem=a_send_sem.at[step],
            recv_sem=a_recv_sem.at[me],
            device_id=(dp, to),
            device_id_type=MESH,
        )

    def a_arrived(step):
        origin = (me + 8 - step) % 8
        return pltpu.make_async_remote_copy(
            src_ref=a_send.at[pl.ds(0, SLOT), :],
            dst_ref=a_recv.at[origin],
            send_sem=a_send_sem.at[step],
            recv_sem=a_recv_sem.at[origin],
            device_id=(dp, origin),
            device_id_type=MESH,
        )

    for step in range(1, 8):
        a_copy(step).start()
    a_recv[me] = a_send[pl.ds(pl.multiple_of(me * SLOT, SLOT), SLOT), :]
    finish(CHUNKS - 2)
    drain_some(CHUNKS - 4, CHUNKS - 3)
    for step in range(1, 8):
        a_arrived(step).wait_recv()
    h_copy = sibling_copy(a_recv, sib_recv, h_sem)
    h_copy.start()
    finish(CHUNKS - 1)
    drain_some(CHUNKS - 3, CHUNKS - 1)
    h_copy.wait_recv()
    for t in range(8):
        for k in range(2):
            at = (t % 2) * 2 * half + k * half
            piece = jnp.where(core == k, a_recv[t], sib_recv[t])
            grads_out[:, t // 2, at : at + half] = piece[0:entries]

    h_copy.wait_send()
    b_copy.wait_send()
    rows_copy.wait_send()
    for step in range(1, 8):
        a_copy(step).wait_send()

    drain_some(CHUNKS - 1, CHUNKS)


def fused(
    embedded,
    resid_grad,
    query_grad,
    query_weight,
    ngram_rows,
    touched_rows,
    row_values,
    row_mean,
    row_square,
):
    micro, group, width = embedded.shape
    hidden = query_grad.shape[2]
    tables = touched_rows.shape[0]
    entries = touched_rows.shape[2]
    cols, half, rows = hidden // CHUNKS, width // 2, width // 2
    slots = tables * SLOT
    f32, bf16, i16 = jnp.float32, jnp.bfloat16, jnp.int16
    dma = pltpu.SemaphoreType.DMA
    vmem = pltpu.VMEM
    anywhere = pl.BlockSpec(memory_space=pl.ANY)
    in_hbm = pl.BlockSpec(memory_space=pltpu.HBM)
    in_vmem = pl.BlockSpec(memory_space=pltpu.VMEM)
    operands = (embedded, resid_grad, query_grad, query_weight, ngram_rows.transpose(0, 2, 1), touched_rows)
    operands = [pltpu.with_memory_space_constraint(operand, pltpu.HBM) for operand in operands]
    weight_grad, grads, lists = pl.pallas_call(
        kernel,
        out_shape=(
            jax.ShapeDtypeStruct((width, hidden), f32),
            jax.ShapeDtypeStruct((entries, SLICES, SW), f32),
            jax.ShapeDtypeStruct((entries, SLICES, SW), f32),
        ),
        in_specs=[in_hbm] * 6,
        out_specs=(anywhere, in_vmem, in_vmem),
        scratch_shapes=[
            vmem((micro, SLICES, group), jnp.int32),
            vmem(touched_rows.shape, jnp.int32),
            vmem((128, 128), f32),
            vmem((micro, group, width), bf16),
            vmem((width + slots, micro * group), bf16),
            vmem((micro, group, width), bf16),
            vmem((width, hidden), bf16),
            vmem((CHUNKS, micro, group, cols), bf16),
            vmem((CHUNKS, width + slots, cols), f32),
            vmem((CHUNKS, rows, cols), f32),
            vmem((CHUNKS, rows, cols), i16),
            vmem((CHUNKS, rows, cols), i16),
            vmem((CHUNKS, 8, cols), f32),
            vmem((CHUNKS, 8, cols), f32),
            vmem((CHUNKS, rows, cols), f32),
            vmem((slots, width), f32),
            vmem((slots, half), f32),
            vmem((slots, half), f32),
            vmem((slots, half), f32),
            vmem((slots, half), f32),
            vmem((slots, half), f32),
            vmem((tables, SLOT, half), f32),
            vmem((tables, SLOT, half), f32),
            dma((5 + CHUNKS,)),
            dma((CHUNKS, tables, 3)),
            dma((CHUNKS, tables)),
            dma((CHUNKS, 2)),
            dma((CHUNKS, 2)),
            dma((CHUNKS, 2)),
            dma((CHUNKS, 2)),
            dma((CHUNKS,)),
            dma((2,)),
            dma((2,)),
            dma((tables,)),
            dma((tables,)),
            dma((2,)),
        ],
        compiler_params=pltpu.CompilerParams(
            collective_id=0, has_side_effects=True, vmem_limit_bytes=40 * 1024 * 1024
        ),
        cost_estimate=pl.CostEstimate(flops=3 * 10**9, bytes_accessed=2 * 10**7, transcendentals=0),
    )(*operands)

    def turned(rows):
        return rows[0].transpose(1, 0, 2)

    after = adam_rows(grads, turned(row_values), turned(row_mean), turned(row_square), lists >= 0)
    values_next, mean_next, square_next = [rows.transpose(1, 0, 2)[None] for rows in after]
    return (weight_grad, values_next, mean_next, square_next)


def solution(mesh):
    placed = (
        P(None, "dp", "table"),
        P(None, "dp", "table"),
        P(None, ("dp", "table"), None),
        P("table", None),
        P(None, "dp", None),
        P(),
        P("table", None, None, None),
        P("table", None, None, None),
        P("table", None, None, None),
    )
    fits = mesh.shape["dp"] == 4 and mesh.shape["table"] == 8
    return jax.shard_map(
        fused if fits else local,
        mesh=mesh,
        in_specs=placed,
        out_specs=(
            P("table", None),
            P("table", None, None, None),
            P("table", None, None, None),
            P("table", None, None, None),
        ),
        check_vma=False,
    )
```

```python
import functools

import jax
import jax.numpy as jnp
from jax import lax
from jax.experimental import pallas as pl
from jax.experimental.pallas import tpu as pltpu
from jax.sharding import PartitionSpec as P

SLICES = 4
SW = 1024


beta_one = 0.9
beta_two = 0.95
learn_rate = 0.01
adam_eps = 1e-08
adam_step = 10


def adam_rows(grads, values, mean, square, live):
    corr_one = 1.0 - beta_one**adam_step
    corr_two = 1.0 - beta_two**adam_step
    mean_next = beta_one * mean + (1.0 - beta_one) * grads
    square_next = beta_two * square + (1.0 - beta_two) * grads * grads
    update = learn_rate * (mean_next / corr_one) / (jnp.sqrt(square_next / corr_two) + adam_eps)
    values_next = values - update
    return (
        jnp.where(live, values_next, values),
        jnp.where(live, mean_next, mean),
        jnp.where(live, square_next, square),
    )


def make_step(emb_part, weight_part, carry, piece):
    back_part, wgrad = carry
    back = jnp.einsum("mrh,ph->mrp", piece, weight_part, preferred_element_type=jnp.float32)
    back_part = back
    wgrad = wgrad + jnp.einsum("mrp,mrh->ph", emb_part, piece, preferred_element_type=jnp.float32)
    return (back_part, wgrad)


def local(
    embedded,
    resid_grad,
    query_grad,
    query_weight,
    ngram_rows,
    touched_rows,
    row_values,
    row_mean,
    row_square,
):
    micro_count, group_tokens, width_part = embedded.shape
    hidden = query_grad.shape[2]
    tables = lax.axis_size("table")
    table_idx = lax.axis_index("table")
    zero_grad = jnp.zeros((width_part, hidden), jnp.float32)
    wgrad = zero_grad
    backs = []
    for micro in range(micro_count):
        start_back = jnp.zeros((1, group_tokens, width_part), jnp.float32)
        back_one, wgrad = make_step(
            embedded[micro : micro + 1],
            query_weight,
            (start_back, wgrad),
            lax.all_gather(query_grad[micro : micro + 1], "table", axis=1, tiled=True),
        )
        backs.append(back_one)
    back_all = jnp.concatenate(backs, axis=0)
    emb_grad = resid_grad.astype(jnp.float32) + back_all
    weight_grad = lax.psum(wgrad, "dp")
    slice_idx = table_idx * width_part // SW
    ids = lax.dynamic_index_in_dim(ngram_rows, slice_idx, 2, False)
    listed = lax.dynamic_index_in_dim(touched_rows, slice_idx, 1, False)
    entries = listed.shape[1]
    flat_list = listed.reshape(tables * entries)
    onehot = (ids[:, :, None] == flat_list[None, None, :]).astype(jnp.float32)
    buckets = jnp.einsum(
        "mtk,mtp->kp",
        onehot,
        emb_grad,
        precision=lax.Precision.HIGHEST,
        preferred_element_type=jnp.float32,
    )
    buckets = buckets.reshape(tables, entries, width_part)
    arrived = lax.all_to_all(buckets, "table", split_axis=0, concat_axis=0, tiled=True)
    per_slice = tables // SLICES
    local_grad = (
        arrived.reshape(SLICES, per_slice, entries, width_part)
        .transpose(0, 2, 1, 3)
        .reshape(SLICES, entries, per_slice * width_part)
    )
    mine = lax.dynamic_index_in_dim(touched_rows, table_idx, 0, False)
    live = (mine >= 0)[..., None]
    values = row_values[0]
    mean = row_mean[0]
    square = row_square[0]
    grads = lax.psum(local_grad, "dp")
    values_next, mean_next, square_next = adam_rows(grads, values, mean, square, live)
    return (weight_grad, values_next[None], mean_next[None], square_next[None])


LEAD = 3
CHUNKS = 8
SLOT = 16
MESH = pl.DeviceIdType.MESH
UP, DOWN, ACROSS, UP_TWO, DOWN_TWO = range(5)
HOPS = (1, -1, 0, 2, -2)


def kernel(
    emb_hbm,
    resid_hbm,
    qg_hbm,
    w_hbm,
    ids_hbm,
    touched_hbm,
    out_hbm,
    grads_out,
    live_out,
    ids,
    touched,
    lists,
    emb,
    left,
    resid,
    w,
    gq,
    prod,
    part_recv,
    q_send,
    q_recv,
    s_send,
    s_recv,
    res,
    bucket,
    b_send,
    b_recv,
    y_send,
    y_recv,
    a_send,
    a_recv,
    sib_recv,
    load_sem,
    g_send_sem,
    g_recv_sem,
    p_sem,
    q_sem,
    s_sem,
    f_sem,
    o_sem,
    b_sem,
    y_sem,
    a_send_sem,
    a_recv_sem,
    h_sem,
):
    dp, me = lax.axis_index("dp"), lax.axis_index("table")
    y, core = dp // 2, dp % 2
    z, x = me // 2, me % 2
    sib = dp + 1 - 2 * core
    ynb = (1 - y) * 2 + core
    zpair = z + 1 - 2 * (z % 2)
    micro, mine, hidden = qg_hbm.shape
    cols = hidden // CHUNKS
    width = emb.shape[2]
    rows = width // 2

    barrier = pltpu.get_barrier_semaphore()
    for step in range(1, 8):
        pl.semaphore_signal(barrier, inc=1, device_id=(dp, (me + step) % 8), device_id_type=MESH)
    pl.semaphore_signal(barrier, inc=1, device_id=(sib, me), device_id_type=MESH)
    pl.semaphore_signal(barrier, inc=1, device_id=(ynb, me), device_id_type=MESH)

    loads = [
        pltpu.make_async_copy(emb_hbm, emb, load_sem.at[0]),
        pltpu.make_async_copy(resid_hbm, resid, load_sem.at[1]),
        pltpu.make_async_copy(w_hbm, w, load_sem.at[2]),
        pltpu.make_async_copy(ids_hbm, ids, load_sem.at[3]),
        pltpu.make_async_copy(touched_hbm, touched, load_sem.at[4]),
    ]

    def span(c):
        return pl.ds(pl.multiple_of(c * cols, cols), cols)

    def tokens(t):
        return pl.ds(pl.multiple_of(t * mine, mine), mine)

    def held(c, t):
        return gq.at[c, :, tokens(t), :]

    def own_load(c):
        return pltpu.make_async_copy(qg_hbm.at[:, :, span(c)], held(c, me), load_sem.at[5 + c])

    for c in range(CHUNKS):
        own_load(c).start()
    pl.semaphore_wait(barrier, 9)

    def shard_copy(c, t, way):
        to = (dp, (z + HOPS[way]) * 2 + x) if way != ACROSS else (dp, z * 2 + 1 - x)
        return pltpu.make_async_remote_copy(
            src_ref=held(c, t),
            dst_ref=held(c, t),
            send_sem=g_send_sem.at[c, t, way],
            recv_sem=g_recv_sem.at[c, t],
            device_id=to,
            device_id_type=MESH,
        )

    def arrived(c, t):
        shard_copy(c, t, ACROSS).wait_recv()

    def each_own(c, act):
        act(shard_copy(c, me, ACROSS))
        for way, there in ((UP, z < 3), (DOWN, z > 0), (UP_TWO, z < 2), (DOWN_TWO, z > 1)):

            @pl.when(there)
            def _():
                act(shard_copy(c, me, way))

    def send_own(c):
        own_load(c).wait()
        each_own(c, start)

    def each_forward(c, far, act, wait):
        for sign, way in ((-1, UP), (1, DOWN)):
            from_z = z + sign * far
            t = from_z * 2 + x
            there = from_z >= 0 if sign < 0 else from_z < 4
            onward = z < 3 if way == UP else z > 0

            @pl.when(there)
            def _():
                if wait:
                    arrived(c, t)

                if far == 2:

                    @pl.when(onward)
                    def _():
                        act(shard_copy(c, t, way))

                if far == 1:

                    @pl.when((c % 2 == 0) | (from_z != zpair))
                    def _():
                        act(shard_copy(c, t, ACROSS))
                else:
                    act(shard_copy(c, t, ACROSS))

    def each_relay(c, act, wait):
        t = z * 2 + 1 - x

        @pl.when(c % 2 == 1)
        def _():
            if wait:
                arrived(c, t)

            @pl.when(z % 2 == 0)
            def _():
                act(shard_copy(c, t, UP))

            @pl.when(z % 2 == 1)
            def _():
                act(shard_copy(c, t, DOWN))

    def start(copy):
        copy.start()

    def sibling_copy(src, dst, sems):
        return pltpu.make_async_remote_copy(
            src_ref=src, dst_ref=dst, send_sem=sems.at[0], recv_sem=sems.at[1], device_id=(sib, me), device_id_type=MESH
        )

    def y_copy(src, dst, sems):
        return pltpu.make_async_remote_copy(
            src_ref=src, dst_ref=dst, send_sem=sems.at[0], recv_sem=sems.at[1], device_id=(ynb, me), device_id_type=MESH
        )

    def part_copy(c):
        return sibling_copy(prod.at[c, 0:rows], part_recv.at[c], p_sem.at[c])

    def q_copy(c):
        return y_copy(q_send.at[c], q_recv.at[c], q_sem.at[c])

    def s_copy(c):
        return y_copy(s_send.at[c], s_recv.at[c], s_sem.at[c])

    def out_rows(k):
        return pl.ds(pl.multiple_of(k * rows, rows), rows)

    def final_copy(c):
        return sibling_copy(res.at[c], out_hbm.at[out_rows(core), span(c)], f_sem.at[c])

    def out_copy(c):
        return pltpu.make_async_copy(res.at[c], out_hbm.at[out_rows(core), span(c)], o_sem.at[c])

    def dot(a, b):
        return jnp.dot(a, b, preferred_element_type=jnp.float32)

    def dot_nt(a, b):
        return lax.dot_general(a, b, (((1,), (1,)), ((), ())), preferred_element_type=jnp.float32)

    def compute(c):
        for far in (1, 2, 3):
            other = (z + far) % 4
            arrived(c, other * 2 + 1 - x)

        @pl.when(c % 2 == 0)
        def _():
            arrived(c, z * 2 + 1 - x)

        block = gq[c].reshape(micro * mine * 8, cols)
        prod[c] = dot(left[...], block)
        part_copy(c).start()
        sums = prod[c, width:, :]
        high = sums.astype(jnp.bfloat16)
        low = (sums - high.astype(jnp.float32)).astype(jnp.bfloat16)
        terms = dot_nt(jnp.concatenate([high, low], axis=0), w[:, span(c)])
        slots = bucket.shape[0]
        bucket[...] += terms[0:slots] + terms[slots : 2 * slots]

    def core_sum(c):
        part_copy(c).wait_recv()
        total = prod[c, rows:width, :] + part_recv[c]
        top = jnp.maximum(jnp.max(jnp.abs(total), axis=0, keepdims=True), 1e-30)
        codes = jnp.round(total * (32767.0 / top))
        q_send[c] = codes.astype(jnp.int32).astype(jnp.int16)
        s_send[c] = jnp.broadcast_to(top * (1.0 / 32767.0), s_send.shape[1:])
        q_copy(c).start()
        s_copy(c).start()

    def finish(c):
        q_copy(c).wait_recv()
        s_copy(c).wait_recv()
        here = q_send[c].astype(jnp.int32).astype(jnp.float32) * s_send[c][0:1, :]
        there = q_recv[c].astype(jnp.int32).astype(jnp.float32) * s_recv[c][0:1, :]
        res[c] = jnp.where(y == 0, here, there) + jnp.where(y == 0, there, here)
        final_copy(c).start()
        out_copy(c).start()

    def guarded(c, stage):
        @pl.when((c >= 0) & (c < CHUNKS))
        def _():
            stage(c)

    def forward_stage(far):
        def stage(c):
            each_forward(c, far, start, True)
            if far == 1:
                each_relay(c, start, True)

        return stage

    for c in range(LEAD):
        send_own(c)
    for at in (4, 3, 1, 0, 2):
        loads[at].start()

    group = mine * 8
    entries = touched.shape[2]
    slice_idx = me * width // SW
    loads[4].wait()
    lists[...] = jnp.full(lists.shape, -1.0, jnp.float32)
    listed = touched[:, 0, :]
    for s in range(1, SLICES):
        listed = jnp.where(slice_idx == s, touched[:, s, :], listed)
    lists[0:8, 0:entries] = listed.astype(jnp.float32)
    lists[8 : 8 + SLICES, 0:entries] = touched[me].astype(jnp.float32)
    columns = lists[...].T
    for s in range(SLICES):
        live_out[:, s, :] = jnp.broadcast_to(columns[0:entries, 8 + s : 9 + s], (entries, live_out.shape[2]))
    loads[3].wait()
    for m in range(micro):
        row = ids[m, pl.ds(slice_idx, 1), :].astype(jnp.float32)
        for o in range(8):
            hit = columns[0:SLOT, o : o + 1] == row
            left[width + o * SLOT : width + (o + 1) * SLOT, m * group : (m + 1) * group] = jnp.where(hit, 1.0, 0.0).astype(jnp.bfloat16)
    loads[1].wait()
    bucket[...] = dot(left[width:, 0:group], resid[0]) + dot(left[width:, group : 2 * group], resid[1])
    loads[0].wait()
    for m in range(micro):
        for k in range(2):
            first = rows * (1 - core) if k == 0 else rows * core
            block = emb[m, :, k * rows : (k + 1) * rows].T
            left[pl.ds(pl.multiple_of(first, rows), rows), m * group : (m + 1) * group] = block
    loads[2].wait()

    def sent(copy):
        copy.wait_send()

    def drain(c):
        each_own(c, sent)
        for far in (1, 2, 3):
            each_forward(c, far, sent, False)
        each_relay(c, sent, False)
        part_copy(c).wait_send()
        q_copy(c).wait_send()
        s_copy(c).wait_send()
        final_copy(c).wait()
        out_copy(c).wait()

    def slot(s, carry):
        guarded(s + LEAD - 1, send_own)
        guarded(s - 1, forward_stage(1))
        guarded(s - 1, forward_stage(2))
        guarded(s - 2, forward_stage(3))
        guarded(s - 3, compute)
        guarded(s - 4, core_sum)
        guarded(s - 6, finish)
        guarded(s - 7, drain)
        return carry

    lax.fori_loop(1, CHUNKS + 2, slot, 0)

    def drain_some(low, high):
        def one(c, carry):
            drain(c)
            return carry

        lax.fori_loop(low, high, one, 0)

    half = b_send.shape[1]

    def half_cols(k):
        return pl.ds(pl.multiple_of(k * half, half), half)

    b_copy = sibling_copy(b_send, b_recv, b_sem)
    compute(CHUNKS - 1)
    b_send[...] = bucket[:, half_cols(1 - core)]
    b_copy.start()
    core_sum(CHUNKS - 2)
    b_copy.wait_recv()
    y_send[...] = bucket[:, half_cols(core)] + b_recv[...]
    rows_copy = y_copy(y_send, y_recv, y_sem)
    rows_copy.start()
    core_sum(CHUNKS - 1)
    finish(CHUNKS - 4)
    drain_some(CHUNKS - 5, CHUNKS - 4)
    finish(CHUNKS - 3)
    rows_copy.wait_recv()
    a_send[...] = y_send[...] + y_recv[...]

    def a_copy(step):
        to = (me + step) % 8
        return pltpu.make_async_remote_copy(
            src_ref=a_send.at[pl.ds(pl.multiple_of(to * SLOT, SLOT), SLOT), :],
            dst_ref=a_recv.at[me],
            send_sem=a_send_sem.at[step],
            recv_sem=a_recv_sem.at[me],
            device_id=(dp, to),
            device_id_type=MESH,
        )

    def a_arrived(step):
        origin = (me + 8 - step) % 8
        return pltpu.make_async_remote_copy(
            src_ref=a_send.at[pl.ds(0, SLOT), :],
            dst_ref=a_recv.at[origin],
            send_sem=a_send_sem.at[step],
            recv_sem=a_recv_sem.at[origin],
            device_id=(dp, origin),
            device_id_type=MESH,
        )

    for step in range(1, 8):
        a_copy(step).start()
    a_recv[me] = a_send[pl.ds(pl.multiple_of(me * SLOT, SLOT), SLOT), :]
    finish(CHUNKS - 2)
    drain_some(CHUNKS - 4, CHUNKS - 3)
    for step in range(1, 8):
        a_arrived(step).wait_recv()
    h_copy = sibling_copy(a_recv, sib_recv, h_sem)
    h_copy.start()
    finish(CHUNKS - 1)
    drain_some(CHUNKS - 3, CHUNKS - 1)
    h_copy.wait_recv()
    for t in range(8):
        for k in range(2):
            at = (t % 2) * 2 * half + k * half
            piece = jnp.where(core == k, a_recv[t], sib_recv[t])
            grads_out[:, t // 2, at : at + half] = piece[0:entries]

    h_copy.wait_send()
    b_copy.wait_send()
    rows_copy.wait_send()
    for step in range(1, 8):
        a_copy(step).wait_send()

    drain_some(CHUNKS - 1, CHUNKS)


def fused(
    embedded,
    resid_grad,
    query_grad,
    query_weight,
    ngram_rows,
    touched_rows,
    row_values,
    row_mean,
    row_square,
):
    micro, group, width = embedded.shape
    hidden = query_grad.shape[2]
    tables = touched_rows.shape[0]
    entries = touched_rows.shape[2]
    cols, half, rows = hidden // CHUNKS, width // 2, width // 2
    slots = tables * SLOT
    f32, bf16, i16 = jnp.float32, jnp.bfloat16, jnp.int16
    dma = pltpu.SemaphoreType.DMA
    vmem = pltpu.VMEM
    anywhere = pl.BlockSpec(memory_space=pl.ANY)
    in_hbm = pl.BlockSpec(memory_space=pltpu.HBM)
    in_vmem = pl.BlockSpec(memory_space=pltpu.VMEM)
    operands = (embedded, resid_grad, query_grad, query_weight, ngram_rows.transpose(0, 2, 1), touched_rows)
    operands = [pltpu.with_memory_space_constraint(operand, pltpu.HBM) for operand in operands]
    weight_grad, grads, lists = pl.pallas_call(
        kernel,
        out_shape=(
            jax.ShapeDtypeStruct((width, hidden), f32),
            jax.ShapeDtypeStruct((entries, SLICES, SW), f32),
            jax.ShapeDtypeStruct((entries, SLICES, SW), f32),
        ),
        in_specs=[in_hbm] * 6,
        out_specs=(anywhere, in_vmem, in_vmem),
        scratch_shapes=[
            vmem((micro, SLICES, group), jnp.int32),
            vmem(touched_rows.shape, jnp.int32),
            vmem((128, 128), f32),
            vmem((micro, group, width), bf16),
            vmem((width + slots, micro * group), bf16),
            vmem((micro, group, width), bf16),
            vmem((width, hidden), bf16),
            vmem((CHUNKS, micro, group, cols), bf16),
            vmem((CHUNKS, width + slots, cols), f32),
            vmem((CHUNKS, rows, cols), f32),
            vmem((CHUNKS, rows, cols), i16),
            vmem((CHUNKS, rows, cols), i16),
            vmem((CHUNKS, 8, cols), f32),
            vmem((CHUNKS, 8, cols), f32),
            vmem((CHUNKS, rows, cols), f32),
            vmem((slots, width), f32),
            vmem((slots, half), f32),
            vmem((slots, half), f32),
            vmem((slots, half), f32),
            vmem((slots, half), f32),
            vmem((slots, half), f32),
            vmem((tables, SLOT, half), f32),
            vmem((tables, SLOT, half), f32),
            dma((5 + CHUNKS,)),
            dma((CHUNKS, tables, 5)),
            dma((CHUNKS, tables)),
            dma((CHUNKS, 2)),
            dma((CHUNKS, 2)),
            dma((CHUNKS, 2)),
            dma((CHUNKS, 2)),
            dma((CHUNKS,)),
            dma((2,)),
            dma((2,)),
            dma((tables,)),
            dma((tables,)),
            dma((2,)),
        ],
        compiler_params=pltpu.CompilerParams(
            collective_id=0, has_side_effects=True, vmem_limit_bytes=40 * 1024 * 1024
        ),
        cost_estimate=pl.CostEstimate(flops=3 * 10**9, bytes_accessed=2 * 10**7, transcendentals=0),
    )(*operands)

    def turned(rows):
        return rows[0].transpose(1, 0, 2)

    after = adam_rows(grads, turned(row_values), turned(row_mean), turned(row_square), lists >= 0)
    values_next, mean_next, square_next = [rows.transpose(1, 0, 2)[None] for rows in after]
    return (weight_grad, values_next, mean_next, square_next)


def solution(mesh):
    placed = (
        P(None, "dp", "table"),
        P(None, "dp", "table"),
        P(None, ("dp", "table"), None),
        P("table", None),
        P(None, "dp", None),
        P(),
        P("table", None, None, None),
        P("table", None, None, None),
        P("table", None, None, None),
    )
    fits = mesh.shape["dp"] == 4 and mesh.shape["table"] == 8
    return jax.shard_map(
        fused if fits else local,
        mesh=mesh,
        in_specs=placed,
        out_specs=(
            P("table", None),
            P("table", None, None, None),
            P("table", None, None, None),
            P("table", None, None, None),
        ),
        check_vma=False,
    )
```

```python
import functools

import jax
import jax.numpy as jnp
from jax import lax
from jax.experimental import pallas as pl
from jax.experimental.pallas import tpu as pltpu
from jax.sharding import PartitionSpec as P

SLICES = 4
SW = 1024


beta_one = 0.9
beta_two = 0.95
learn_rate = 0.01
adam_eps = 1e-08
adam_step = 10


def adam_rows(grads, values, mean, square, live):
    corr_one = 1.0 - beta_one**adam_step
    corr_two = 1.0 - beta_two**adam_step
    mean_next = beta_one * mean + (1.0 - beta_one) * grads
    square_next = beta_two * square + (1.0 - beta_two) * grads * grads
    update = learn_rate * (mean_next / corr_one) / (jnp.sqrt(square_next / corr_two) + adam_eps)
    values_next = values - update
    return (
        jnp.where(live, values_next, values),
        jnp.where(live, mean_next, mean),
        jnp.where(live, square_next, square),
    )


def make_step(emb_part, weight_part, carry, piece):
    back_part, wgrad = carry
    back = jnp.einsum("mrh,ph->mrp", piece, weight_part, preferred_element_type=jnp.float32)
    back_part = back
    wgrad = wgrad + jnp.einsum("mrp,mrh->ph", emb_part, piece, preferred_element_type=jnp.float32)
    return (back_part, wgrad)


def local(
    embedded,
    resid_grad,
    query_grad,
    query_weight,
    ngram_rows,
    touched_rows,
    row_values,
    row_mean,
    row_square,
):
    micro_count, group_tokens, width_part = embedded.shape
    hidden = query_grad.shape[2]
    tables = lax.axis_size("table")
    table_idx = lax.axis_index("table")
    zero_grad = jnp.zeros((width_part, hidden), jnp.float32)
    wgrad = zero_grad
    backs = []
    for micro in range(micro_count):
        start_back = jnp.zeros((1, group_tokens, width_part), jnp.float32)
        back_one, wgrad = make_step(
            embedded[micro : micro + 1],
            query_weight,
            (start_back, wgrad),
            lax.all_gather(query_grad[micro : micro + 1], "table", axis=1, tiled=True),
        )
        backs.append(back_one)
    back_all = jnp.concatenate(backs, axis=0)
    emb_grad = resid_grad.astype(jnp.float32) + back_all
    weight_grad = lax.psum(wgrad, "dp")
    slice_idx = table_idx * width_part // SW
    ids = lax.dynamic_index_in_dim(ngram_rows, slice_idx, 2, False)
    listed = lax.dynamic_index_in_dim(touched_rows, slice_idx, 1, False)
    entries = listed.shape[1]
    flat_list = listed.reshape(tables * entries)
    onehot = (ids[:, :, None] == flat_list[None, None, :]).astype(jnp.float32)
    buckets = jnp.einsum(
        "mtk,mtp->kp",
        onehot,
        emb_grad,
        precision=lax.Precision.HIGHEST,
        preferred_element_type=jnp.float32,
    )
    buckets = buckets.reshape(tables, entries, width_part)
    arrived = lax.all_to_all(buckets, "table", split_axis=0, concat_axis=0, tiled=True)
    per_slice = tables // SLICES
    local_grad = (
        arrived.reshape(SLICES, per_slice, entries, width_part)
        .transpose(0, 2, 1, 3)
        .reshape(SLICES, entries, per_slice * width_part)
    )
    mine = lax.dynamic_index_in_dim(touched_rows, table_idx, 0, False)
    live = (mine >= 0)[..., None]
    values = row_values[0]
    mean = row_mean[0]
    square = row_square[0]
    grads = lax.psum(local_grad, "dp")
    values_next, mean_next, square_next = adam_rows(grads, values, mean, square, live)
    return (weight_grad, values_next[None], mean_next[None], square_next[None])


LEAD = 3
CHUNKS = 8
SLOT = 16
MESH = pl.DeviceIdType.MESH
UP, DOWN, ACROSS = 0, 1, 2


def kernel(
    emb_hbm,
    resid_hbm,
    qg_hbm,
    w_hbm,
    ids_hbm,
    touched_hbm,
    out_hbm,
    grads_out,
    live_out,
    ids,
    touched,
    lists,
    emb,
    left,
    resid,
    w,
    gq,
    prod,
    p_send,
    p_recv,
    ps_send,
    ps_recv,
    q_send,
    q_recv,
    s_send,
    s_recv,
    f_send,
    f_recv,
    fs_send,
    fs_recv,
    res,
    bucket,
    b_send,
    b_recv,
    y_send,
    y_recv,
    a_send,
    a_recv,
    sib_recv,
    load_sem,
    g_send_sem,
    g_recv_sem,
    p_sem,
    ps_sem,
    q_sem,
    s_sem,
    f_sem,
    fs_sem,
    o_sem,
    b_sem,
    y_sem,
    a_send_sem,
    a_recv_sem,
    h_sem,
):
    dp, me = lax.axis_index("dp"), lax.axis_index("table")
    y, core = dp // 2, dp % 2
    z, x = me // 2, me % 2
    sib = dp + 1 - 2 * core
    ynb = (1 - y) * 2 + core
    zpair = z + 1 - 2 * (z % 2)
    micro, mine, hidden = qg_hbm.shape
    cols = hidden // CHUNKS
    width = emb.shape[2]
    rows = width // 2

    barrier = pltpu.get_barrier_semaphore()
    for step in range(1, 8):
        pl.semaphore_signal(barrier, inc=1, device_id=(dp, (me + step) % 8), device_id_type=MESH)
    pl.semaphore_signal(barrier, inc=1, device_id=(sib, me), device_id_type=MESH)
    pl.semaphore_signal(barrier, inc=1, device_id=(ynb, me), device_id_type=MESH)

    loads = [
        pltpu.make_async_copy(emb_hbm, emb, load_sem.at[0]),
        pltpu.make_async_copy(resid_hbm, resid, load_sem.at[1]),
        pltpu.make_async_copy(w_hbm, w, load_sem.at[2]),
        pltpu.make_async_copy(ids_hbm, ids, load_sem.at[3]),
        pltpu.make_async_copy(touched_hbm, touched, load_sem.at[4]),
    ]

    def span(c):
        return pl.ds(pl.multiple_of(c * cols, cols), cols)

    def tokens(t):
        return pl.ds(pl.multiple_of(t * mine, mine), mine)

    def held(c, t):
        return gq.at[c, :, tokens(t), :]

    def own_load(c):
        return pltpu.make_async_copy(qg_hbm.at[:, :, span(c)], held(c, me), load_sem.at[5 + c])

    pl.semaphore_wait(barrier, 9)

    def shard_copy(c, t, way, source=None):
        to_z = z + 1 if way == UP else z - 1
        to = (dp, to_z * 2 + x) if way != ACROSS else (dp, z * 2 + 1 - x)
        return pltpu.make_async_remote_copy(
            src_ref=held(c, t) if source is None else source,
            dst_ref=held(c, t),
            send_sem=g_send_sem.at[c, t, way],
            recv_sem=g_recv_sem.at[c, t],
            device_id=to,
            device_id_type=MESH,
        )

    def arrived(c, t):
        shard_copy(c, t, ACROSS).wait_recv()

    def each_own(c, act):
        own = qg_hbm.at[:, :, span(c)]

        @pl.when(z < 3)
        def _():
            act(shard_copy(c, me, UP, own))

        @pl.when(z > 0)
        def _():
            act(shard_copy(c, me, DOWN, own))

        act(shard_copy(c, me, ACROSS, own))

    def each_forward(c, far, act, wait):
        for sign, way in ((-1, UP), (1, DOWN)):
            from_z = z + sign * far
            t = from_z * 2 + x
            there = from_z >= 0 if sign < 0 else from_z < 4
            onward = z < 3 if way == UP else z > 0

            @pl.when(there)
            def _():
                if wait:
                    arrived(c, t)

                @pl.when(onward)
                def _():
                    act(shard_copy(c, t, way))

                if far == 1:

                    @pl.when((c % 2 == 0) | (from_z != zpair))
                    def _():
                        act(shard_copy(c, t, ACROSS))
                else:
                    act(shard_copy(c, t, ACROSS))

    def each_relay(c, act, wait):
        t = z * 2 + 1 - x

        @pl.when(c % 2 == 1)
        def _():
            if wait:
                arrived(c, t)

            @pl.when(z % 2 == 0)
            def _():
                act(shard_copy(c, t, UP))

            @pl.when(z % 2 == 1)
            def _():
                act(shard_copy(c, t, DOWN))

    def start(copy):
        copy.start()

    def sibling_copy(src, dst, sems):
        return pltpu.make_async_remote_copy(
            src_ref=src, dst_ref=dst, send_sem=sems.at[0], recv_sem=sems.at[1], device_id=(sib, me), device_id_type=MESH
        )

    def y_copy(src, dst, sems):
        return pltpu.make_async_remote_copy(
            src_ref=src, dst_ref=dst, send_sem=sems.at[0], recv_sem=sems.at[1], device_id=(ynb, me), device_id_type=MESH
        )

    def part_copies(c):
        return sibling_copy(p_send.at[c], p_recv.at[c], p_sem.at[c]), sibling_copy(ps_send.at[c], ps_recv.at[c], ps_sem.at[c])

    def final_copies(c):
        return sibling_copy(f_send.at[c], f_recv.at[c], f_sem.at[c]), sibling_copy(fs_send.at[c], fs_recv.at[c], fs_sem.at[c])

    def q_copy(c):
        return y_copy(q_send.at[c], q_recv.at[c], q_sem.at[c])

    def s_copy(c):
        return y_copy(s_send.at[c], s_recv.at[c], s_sem.at[c])

    def out_rows(k):
        return pl.ds(pl.multiple_of(k * rows, rows), rows)

    def out_copy(c, k):
        half_rows = out_rows(core if k == 0 else 1 - core)
        return pltpu.make_async_copy(res.at[c, k], out_hbm.at[half_rows, span(c)], o_sem.at[c, k])

    def encode(total, codes, scales):
        top = jnp.maximum(jnp.max(jnp.abs(total), axis=0, keepdims=True), 1e-30)
        codes[...] = jnp.round(total * (32767.0 / top)).astype(jnp.int32).astype(jnp.int16)
        scales[...] = jnp.broadcast_to(top * (1.0 / 32767.0), scales.shape)

    def decode(codes, scales):
        return codes[...].astype(jnp.int32).astype(jnp.float32) * scales[0:1, :]

    def dot(a, b):
        return jnp.dot(a, b, preferred_element_type=jnp.float32)

    def dot_nt(a, b):
        return lax.dot_general(a, b, (((1,), (1,)), ((), ())), preferred_element_type=jnp.float32)

    def compute(c):
        for far in (1, 2, 3):
            other = (z + far) % 4
            arrived(c, other * 2 + 1 - x)

        @pl.when(c % 2 == 0)
        def _():
            arrived(c, z * 2 + 1 - x)

        own_load(c).wait()
        block = gq[c].reshape(micro * mine * 8, cols)
        prod[c] = dot(left[...], block)
        encode(prod[c, 0:rows, :], p_send.at[c], ps_send.at[c])
        for copy in part_copies(c):
            copy.start()
        sums = prod[c, width:, :]
        high = sums.astype(jnp.bfloat16)
        low = (sums - high.astype(jnp.float32)).astype(jnp.bfloat16)
        terms = dot_nt(jnp.concatenate([high, low], axis=0), w[:, span(c)])
        slots = bucket.shape[0]
        bucket[...] += terms[0:slots] + terms[slots : 2 * slots]

    def core_sum(c):
        for copy in part_copies(c):
            copy.wait_recv()
        total = prod[c, rows:width, :] + decode(p_recv.at[c], ps_recv.at[c])
        encode(total, q_send.at[c], s_send.at[c])
        q_copy(c).start()
        s_copy(c).start()

    def finish(c):
        q_copy(c).wait_recv()
        s_copy(c).wait_recv()
        here = decode(q_send.at[c], s_send.at[c])
        there = decode(q_recv.at[c], s_recv.at[c])
        total = jnp.where(y == 0, here, there) + jnp.where(y == 0, there, here)
        encode(total, f_send.at[c], fs_send.at[c])
        for copy in final_copies(c):
            copy.start()
        res[c, 0] = decode(f_send.at[c], fs_send.at[c])
        out_copy(c, 0).start()

    def take(c):
        for copy in final_copies(c):
            copy.wait_recv()
        res[c, 1] = decode(f_recv.at[c], fs_recv.at[c])
        out_copy(c, 1).start()

    def guarded(c, stage):
        @pl.when((c >= 0) & (c < CHUNKS))
        def _():
            stage(c)

    def forward_stage(far):
        def stage(c):
            each_forward(c, far, start, True)
            if far == 1:
                each_relay(c, start, True)

        return stage

    for c in range(LEAD):
        each_own(c, start)
    for at in (4, 3, 1, 0, 2):
        loads[at].start()
    for c in range(CHUNKS):
        own_load(c).start()

    group = mine * 8
    entries = touched.shape[2]
    slice_idx = me * width // SW
    loads[4].wait()
    lists[...] = jnp.full(lists.shape, -1.0, jnp.float32)
    listed = touched[:, 0, :]
    for s in range(1, SLICES):
        listed = jnp.where(slice_idx == s, touched[:, s, :], listed)
    lists[0:8, 0:entries] = listed.astype(jnp.float32)
    lists[8 : 8 + SLICES, 0:entries] = touched[me].astype(jnp.float32)
    columns = lists[...].T
    for s in range(SLICES):
        live_out[:, s, :] = jnp.broadcast_to(columns[0:entries, 8 + s : 9 + s], (entries, live_out.shape[2]))
    loads[3].wait()
    for m in range(micro):
        row = ids[m, pl.ds(slice_idx, 1), :].astype(jnp.float32)
        for o in range(8):
            hit = columns[0:SLOT, o : o + 1] == row
            left[width + o * SLOT : width + (o + 1) * SLOT, m * group : (m + 1) * group] = jnp.where(hit, 1.0, 0.0).astype(jnp.bfloat16)
    loads[1].wait()
    bucket[...] = dot(left[width:, 0:group], resid[0]) + dot(left[width:, group : 2 * group], resid[1])
    loads[0].wait()
    for m in range(micro):
        for k in range(2):
            first = rows * (1 - core) if k == 0 else rows * core
            block = emb[m, :, k * rows : (k + 1) * rows].T
            left[pl.ds(pl.multiple_of(first, rows), rows), m * group : (m + 1) * group] = block
    loads[2].wait()

    def sent(copy):
        copy.wait_send()

    def drain(c):
        each_own(c, sent)
        for far in (1, 2, 3):
            each_forward(c, far, sent, False)
        each_relay(c, sent, False)
        for copy in (*part_copies(c), q_copy(c), s_copy(c), *final_copies(c)):
            copy.wait_send()
        for k in range(2):
            out_copy(c, k).wait()

    def slot(s, carry):
        guarded(s + LEAD - 1, lambda c: each_own(c, start))
        guarded(s - 1, forward_stage(1))
        guarded(s - 2, forward_stage(2))
        guarded(s - 3, forward_stage(3))
        guarded(s - 4, compute)
        guarded(s - 5, core_sum)
        guarded(s - 7, finish)
        guarded(s - 8, take)
        guarded(s - 9, drain)
        return carry

    lax.fori_loop(1, CHUNKS + 3, slot, 0)

    def drain_some(low, high):
        def one(c, carry):
            drain(c)
            return carry

        lax.fori_loop(low, high, one, 0)

    half = b_send.shape[1]

    def half_cols(k):
        return pl.ds(pl.multiple_of(k * half, half), half)

    b_copy = sibling_copy(b_send, b_recv, b_sem)
    compute(CHUNKS - 1)
    b_send[...] = bucket[:, half_cols(1 - core)]
    b_copy.start()
    core_sum(CHUNKS - 2)
    b_copy.wait_recv()
    y_send[...] = bucket[:, half_cols(core)] + b_recv[...]
    rows_copy = y_copy(y_send, y_recv, y_sem)
    rows_copy.start()
    core_sum(CHUNKS - 1)
    finish(CHUNKS - 4)
    take(CHUNKS - 5)
    drain_some(CHUNKS - 6, CHUNKS - 5)
    finish(CHUNKS - 3)
    take(CHUNKS - 4)
    rows_copy.wait_recv()
    a_send[...] = y_send[...] + y_recv[...]

    def a_copy(step):
        to = (me + step) % 8
        return pltpu.make_async_remote_copy(
            src_ref=a_send.at[pl.ds(pl.multiple_of(to * SLOT, SLOT), SLOT), :],
            dst_ref=a_recv.at[me],
            send_sem=a_send_sem.at[step],
            recv_sem=a_recv_sem.at[me],
            device_id=(dp, to),
            device_id_type=MESH,
        )

    def a_arrived(step):
        origin = (me + 8 - step) % 8
        return pltpu.make_async_remote_copy(
            src_ref=a_send.at[pl.ds(0, SLOT), :],
            dst_ref=a_recv.at[origin],
            send_sem=a_send_sem.at[step],
            recv_sem=a_recv_sem.at[origin],
            device_id=(dp, origin),
            device_id_type=MESH,
        )

    for step in range(1, 8):
        a_copy(step).start()
    a_recv[me] = a_send[pl.ds(pl.multiple_of(me * SLOT, SLOT), SLOT), :]
    finish(CHUNKS - 2)
    take(CHUNKS - 3)
    drain_some(CHUNKS - 5, CHUNKS - 3)
    for step in range(1, 8):
        a_arrived(step).wait_recv()
    h_copy = sibling_copy(a_recv, sib_recv, h_sem)
    h_copy.start()
    finish(CHUNKS - 1)
    take(CHUNKS - 2)
    drain_some(CHUNKS - 3, CHUNKS - 2)
    h_copy.wait_recv()
    for t in range(8):
        for k in range(2):
            at = (t % 2) * 2 * half + k * half
            piece = jnp.where(core == k, a_recv[t], sib_recv[t])
            grads_out[:, t // 2, at : at + half] = piece[0:entries]

    h_copy.wait_send()
    b_copy.wait_send()
    rows_copy.wait_send()
    for step in range(1, 8):
        a_copy(step).wait_send()

    take(CHUNKS - 1)
    drain_some(CHUNKS - 2, CHUNKS)


def fused(
    embedded,
    resid_grad,
    query_grad,
    query_weight,
    ngram_rows,
    touched_rows,
    row_values,
    row_mean,
    row_square,
):
    micro, group, width = embedded.shape
    hidden = query_grad.shape[2]
    tables = touched_rows.shape[0]
    entries = touched_rows.shape[2]
    cols, half, rows = hidden // CHUNKS, width // 2, width // 2
    slots = tables * SLOT
    f32, bf16, i16 = jnp.float32, jnp.bfloat16, jnp.int16
    dma = pltpu.SemaphoreType.DMA
    vmem = pltpu.VMEM
    anywhere = pl.BlockSpec(memory_space=pl.ANY)
    in_hbm = pl.BlockSpec(memory_space=pltpu.HBM)
    in_vmem = pl.BlockSpec(memory_space=pltpu.VMEM)
    operands = (embedded, resid_grad, query_grad, query_weight, ngram_rows.transpose(0, 2, 1), touched_rows)
    operands = [pltpu.with_memory_space_constraint(operand, pltpu.HBM) for operand in operands]
    weight_grad, grads, lists = pl.pallas_call(
        kernel,
        out_shape=(
            jax.ShapeDtypeStruct((width, hidden), f32),
            jax.ShapeDtypeStruct((entries, SLICES, SW), f32),
            jax.ShapeDtypeStruct((entries, SLICES, SW), f32),
        ),
        in_specs=[in_hbm] * 6,
        out_specs=(anywhere, in_vmem, in_vmem),
        scratch_shapes=[
            vmem((micro, SLICES, group), jnp.int32),
            vmem(touched_rows.shape, jnp.int32),
            vmem((128, 128), f32),
            vmem((micro, group, width), bf16),
            vmem((width + slots, micro * group), bf16),
            vmem((micro, group, width), bf16),
            vmem((width, hidden), bf16),
            vmem((CHUNKS, micro, group, cols), bf16),
            vmem((CHUNKS, width + slots, cols), f32),
            *[vmem((CHUNKS, rows, cols), i16), vmem((CHUNKS, rows, cols), i16)],
            *[vmem((CHUNKS, 8, cols), f32), vmem((CHUNKS, 8, cols), f32)],
            *[vmem((CHUNKS, rows, cols), i16), vmem((CHUNKS, rows, cols), i16)],
            *[vmem((CHUNKS, 8, cols), f32), vmem((CHUNKS, 8, cols), f32)],
            *[vmem((CHUNKS, rows, cols), i16), vmem((CHUNKS, rows, cols), i16)],
            *[vmem((CHUNKS, 8, cols), f32), vmem((CHUNKS, 8, cols), f32)],
            vmem((CHUNKS, 2, rows, cols), f32),
            vmem((slots, width), f32),
            vmem((slots, half), f32),
            vmem((slots, half), f32),
            vmem((slots, half), f32),
            vmem((slots, half), f32),
            vmem((slots, half), f32),
            vmem((tables, SLOT, half), f32),
            vmem((tables, SLOT, half), f32),
            dma((5 + CHUNKS,)),
            dma((CHUNKS, tables, 3)),
            dma((CHUNKS, tables)),
            *[dma((CHUNKS, 2)) for _ in range(7)],
            dma((2,)),
            dma((2,)),
            dma((tables,)),
            dma((tables,)),
            dma((2,)),
        ],
        compiler_params=pltpu.CompilerParams(
            collective_id=0, has_side_effects=True, vmem_limit_bytes=40 * 1024 * 1024
        ),
        cost_estimate=pl.CostEstimate(flops=3 * 10**9, bytes_accessed=2 * 10**7, transcendentals=0),
    )(*operands)

    def turned(rows):
        return rows[0].transpose(1, 0, 2)

    after = adam_rows(grads, turned(row_values), turned(row_mean), turned(row_square), lists >= 0)
    values_next, mean_next, square_next = [rows.transpose(1, 0, 2)[None] for rows in after]
    return (weight_grad, values_next, mean_next, square_next)


def solution(mesh):
    placed = (
        P(None, "dp", "table"),
        P(None, "dp", "table"),
        P(None, ("dp", "table"), None),
        P("table", None),
        P(None, "dp", None),
        P(),
        P("table", None, None, None),
        P("table", None, None, None),
        P("table", None, None, None),
    )
    fits = mesh.shape["dp"] == 4 and mesh.shape["table"] == 8
    return jax.shard_map(
        fused if fits else local,
        mesh=mesh,
        in_specs=placed,
        out_specs=(
            P("table", None),
            P("table", None, None, None),
            P("table", None, None, None),
            P("table", None, None, None),
        ),
        check_vma=False,
    )
```

```python
import functools

import jax
import jax.numpy as jnp
from jax import lax
from jax.experimental import pallas as pl
from jax.experimental.pallas import tpu as pltpu
from jax.sharding import PartitionSpec as P

SLICES = 4
SW = 1024


beta_one = 0.9
beta_two = 0.95
learn_rate = 0.01
adam_eps = 1e-08
adam_step = 10


def adam_rows(grads, values, mean, square, live):
    corr_one = 1.0 - beta_one**adam_step
    corr_two = 1.0 - beta_two**adam_step
    mean_next = beta_one * mean + (1.0 - beta_one) * grads
    square_next = beta_two * square + (1.0 - beta_two) * grads * grads
    update = learn_rate * (mean_next / corr_one) / (jnp.sqrt(square_next / corr_two) + adam_eps)
    values_next = values - update
    return (
        jnp.where(live, values_next, values),
        jnp.where(live, mean_next, mean),
        jnp.where(live, square_next, square),
    )


def make_step(emb_part, weight_part, carry, piece):
    back_part, wgrad = carry
    back = jnp.einsum("mrh,ph->mrp", piece, weight_part, preferred_element_type=jnp.float32)
    back_part = back
    wgrad = wgrad + jnp.einsum("mrp,mrh->ph", emb_part, piece, preferred_element_type=jnp.float32)
    return (back_part, wgrad)


def local(
    embedded,
    resid_grad,
    query_grad,
    query_weight,
    ngram_rows,
    touched_rows,
    row_values,
    row_mean,
    row_square,
):
    micro_count, group_tokens, width_part = embedded.shape
    hidden = query_grad.shape[2]
    tables = lax.axis_size("table")
    table_idx = lax.axis_index("table")
    zero_grad = jnp.zeros((width_part, hidden), jnp.float32)
    wgrad = zero_grad
    backs = []
    for micro in range(micro_count):
        start_back = jnp.zeros((1, group_tokens, width_part), jnp.float32)
        back_one, wgrad = make_step(
            embedded[micro : micro + 1],
            query_weight,
            (start_back, wgrad),
            lax.all_gather(query_grad[micro : micro + 1], "table", axis=1, tiled=True),
        )
        backs.append(back_one)
    back_all = jnp.concatenate(backs, axis=0)
    emb_grad = resid_grad.astype(jnp.float32) + back_all
    weight_grad = lax.psum(wgrad, "dp")
    slice_idx = table_idx * width_part // SW
    ids = lax.dynamic_index_in_dim(ngram_rows, slice_idx, 2, False)
    listed = lax.dynamic_index_in_dim(touched_rows, slice_idx, 1, False)
    entries = listed.shape[1]
    flat_list = listed.reshape(tables * entries)
    onehot = (ids[:, :, None] == flat_list[None, None, :]).astype(jnp.float32)
    buckets = jnp.einsum(
        "mtk,mtp->kp",
        onehot,
        emb_grad,
        precision=lax.Precision.HIGHEST,
        preferred_element_type=jnp.float32,
    )
    buckets = buckets.reshape(tables, entries, width_part)
    arrived = lax.all_to_all(buckets, "table", split_axis=0, concat_axis=0, tiled=True)
    per_slice = tables // SLICES
    local_grad = (
        arrived.reshape(SLICES, per_slice, entries, width_part)
        .transpose(0, 2, 1, 3)
        .reshape(SLICES, entries, per_slice * width_part)
    )
    mine = lax.dynamic_index_in_dim(touched_rows, table_idx, 0, False)
    live = (mine >= 0)[..., None]
    values = row_values[0]
    mean = row_mean[0]
    square = row_square[0]
    grads = lax.psum(local_grad, "dp")
    values_next, mean_next, square_next = adam_rows(grads, values, mean, square, live)
    return (weight_grad, values_next[None], mean_next[None], square_next[None])


LEAD = 3
CHUNKS = 4
SLOT = 16
MESH = pl.DeviceIdType.MESH
UP, DOWN, ACROSS = 0, 1, 2


def kernel(
    emb_hbm,
    resid_hbm,
    qg_hbm,
    w_hbm,
    ids_hbm,
    touched_hbm,
    out_hbm,
    grads_out,
    live_out,
    ids,
    touched,
    lists,
    emb,
    left,
    resid,
    w,
    gq,
    prod,
    part_recv,
    q_send,
    q_recv,
    s_send,
    s_recv,
    res,
    bucket,
    b_send,
    b_recv,
    y_send,
    y_recv,
    a_send,
    a_recv,
    sib_recv,
    load_sem,
    g_send_sem,
    g_recv_sem,
    p_sem,
    q_sem,
    s_sem,
    f_sem,
    o_sem,
    b_sem,
    y_sem,
    a_send_sem,
    a_recv_sem,
    h_sem,
):
    dp, me = lax.axis_index("dp"), lax.axis_index("table")
    y, core = dp // 2, dp % 2
    z, x = me // 2, me % 2
    sib = dp + 1 - 2 * core
    ynb = (1 - y) * 2 + core
    zpair = z + 1 - 2 * (z % 2)
    micro, mine, hidden = qg_hbm.shape
    cols = hidden // CHUNKS
    width = emb.shape[2]
    rows = width // 2

    barrier = pltpu.get_barrier_semaphore()
    for step in range(1, 8):
        pl.semaphore_signal(barrier, inc=1, device_id=(dp, (me + step) % 8), device_id_type=MESH)
    pl.semaphore_signal(barrier, inc=1, device_id=(sib, me), device_id_type=MESH)
    pl.semaphore_signal(barrier, inc=1, device_id=(ynb, me), device_id_type=MESH)

    loads = [
        pltpu.make_async_copy(emb_hbm, emb, load_sem.at[0]),
        pltpu.make_async_copy(resid_hbm, resid, load_sem.at[1]),
        pltpu.make_async_copy(w_hbm, w, load_sem.at[2]),
        pltpu.make_async_copy(ids_hbm, ids, load_sem.at[3]),
        pltpu.make_async_copy(touched_hbm, touched, load_sem.at[4]),
    ]

    def span(c):
        return pl.ds(pl.multiple_of(c * cols, cols), cols)

    def tokens(t):
        return pl.ds(pl.multiple_of(t * mine, mine), mine)

    def held(c, t):
        return gq.at[c, :, tokens(t), :]

    def own_load(c):
        return pltpu.make_async_copy(qg_hbm.at[:, :, span(c)], held(c, me), load_sem.at[5 + c])

    pl.semaphore_wait(barrier, 9)

    def shard_copy(c, t, way, source=None):
        to_z = z + 1 if way == UP else z - 1
        to = (dp, to_z * 2 + x) if way != ACROSS else (dp, z * 2 + 1 - x)
        return pltpu.make_async_remote_copy(
            src_ref=held(c, t) if source is None else source,
            dst_ref=held(c, t),
            send_sem=g_send_sem.at[c, t, way],
            recv_sem=g_recv_sem.at[c, t],
            device_id=to,
            device_id_type=MESH,
        )

    def arrived(c, t):
        shard_copy(c, t, ACROSS).wait_recv()

    def each_own(c, act):
        own = qg_hbm.at[:, :, span(c)]

        @pl.when(z < 3)
        def _():
            act(shard_copy(c, me, UP, own))

        @pl.when(z > 0)
        def _():
            act(shard_copy(c, me, DOWN, own))

        act(shard_copy(c, me, ACROSS, own))

    def each_forward(c, far, act, wait):
        for sign, way in ((-1, UP), (1, DOWN)):
            from_z = z + sign * far
            t = from_z * 2 + x
            there = from_z >= 0 if sign < 0 else from_z < 4
            onward = z < 3 if way == UP else z > 0

            @pl.when(there)
            def _():
                if wait:
                    arrived(c, t)

                @pl.when(onward)
                def _():
                    act(shard_copy(c, t, way))

                if far == 1:

                    @pl.when((c % 2 == 0) | (from_z != zpair))
                    def _():
                        act(shard_copy(c, t, ACROSS))
                else:
                    act(shard_copy(c, t, ACROSS))

    def each_relay(c, act, wait):
        t = z * 2 + 1 - x

        @pl.when(c % 2 == 1)
        def _():
            if wait:
                arrived(c, t)

            @pl.when(z % 2 == 0)
            def _():
                act(shard_copy(c, t, UP))

            @pl.when(z % 2 == 1)
            def _():
                act(shard_copy(c, t, DOWN))

    def start(copy):
        copy.start()

    def sibling_copy(src, dst, sems):
        return pltpu.make_async_remote_copy(
            src_ref=src, dst_ref=dst, send_sem=sems.at[0], recv_sem=sems.at[1], device_id=(sib, me), device_id_type=MESH
        )

    def y_copy(src, dst, sems):
        return pltpu.make_async_remote_copy(
            src_ref=src, dst_ref=dst, send_sem=sems.at[0], recv_sem=sems.at[1], device_id=(ynb, me), device_id_type=MESH
        )

    def part_copy(c):
        return sibling_copy(prod.at[c, 0:rows], part_recv.at[c], p_sem.at[c])

    def q_copy(c):
        return y_copy(q_send.at[c], q_recv.at[c], q_sem.at[c])

    def s_copy(c):
        return y_copy(s_send.at[c], s_recv.at[c], s_sem.at[c])

    def out_rows(k):
        return pl.ds(pl.multiple_of(k * rows, rows), rows)

    def final_copy(c):
        return sibling_copy(res.at[c], out_hbm.at[out_rows(core), span(c)], f_sem.at[c])

    def out_copy(c):
        return pltpu.make_async_copy(res.at[c], out_hbm.at[out_rows(core), span(c)], o_sem.at[c])

    def dot(a, b):
        return jnp.dot(a, b, preferred_element_type=jnp.float32)

    def dot_nt(a, b):
        return lax.dot_general(a, b, (((1,), (1,)), ((), ())), preferred_element_type=jnp.float32)

    def compute(c):
        for far in (1, 2, 3):
            other = (z + far) % 4
            arrived(c, other * 2 + 1 - x)

        @pl.when(c % 2 == 0)
        def _():
            arrived(c, z * 2 + 1 - x)

        own_load(c).wait()
        block = gq[c].reshape(micro * mine * 8, cols)
        prod[c] = dot(left[...], block)
        part_copy(c).start()
        sums = prod[c, width:, :]
        high = sums.astype(jnp.bfloat16)
        low = (sums - high.astype(jnp.float32)).astype(jnp.bfloat16)
        terms = dot_nt(jnp.concatenate([high, low], axis=0), w[:, span(c)])
        slots = bucket.shape[0]
        bucket[...] += terms[0:slots] + terms[slots : 2 * slots]

    def core_sum(c):
        part_copy(c).wait_recv()
        total = prod[c, rows:width, :] + part_recv[c]
        top = jnp.maximum(jnp.max(jnp.abs(total), axis=0, keepdims=True), 1e-30)
        codes = jnp.round(total * (32767.0 / top))
        q_send[c] = codes.astype(jnp.int32).astype(jnp.int16)
        s_send[c] = jnp.broadcast_to(top * (1.0 / 32767.0), s_send.shape[1:])
        q_copy(c).start()
        s_copy(c).start()

    def finish(c):
        q_copy(c).wait_recv()
        s_copy(c).wait_recv()
        here = q_send[c].astype(jnp.int32).astype(jnp.float32) * s_send[c][0:1, :]
        there = q_recv[c].astype(jnp.int32).astype(jnp.float32) * s_recv[c][0:1, :]
        res[c] = jnp.where(y == 0, here, there) + jnp.where(y == 0, there, here)
        final_copy(c).start()
        out_copy(c).start()

    def guarded(c, stage):
        @pl.when((c >= 0) & (c < CHUNKS))
        def _():
            stage(c)

    def forward_stage(far):
        def stage(c):
            each_forward(c, far, start, True)
            if far == 1:
                each_relay(c, start, True)

        return stage

    for c in range(LEAD):
        each_own(c, start)
    for at in (4, 3, 1, 0, 2):
        loads[at].start()
    for c in range(CHUNKS):
        own_load(c).start()

    group = mine * 8
    entries = touched.shape[2]
    slice_idx = me * width // SW
    loads[4].wait()
    lists[...] = jnp.full(lists.shape, -1.0, jnp.float32)
    listed = touched[:, 0, :]
    for s in range(1, SLICES):
        listed = jnp.where(slice_idx == s, touched[:, s, :], listed)
    lists[0:8, 0:entries] = listed.astype(jnp.float32)
    lists[8 : 8 + SLICES, 0:entries] = touched[me].astype(jnp.float32)
    columns = lists[...].T
    for s in range(SLICES):
        live_out[:, s, :] = jnp.broadcast_to(columns[0:entries, 8 + s : 9 + s], (entries, live_out.shape[2]))
    loads[3].wait()
    for m in range(micro):
        row = ids[m, pl.ds(slice_idx, 1), :].astype(jnp.float32)
        for o in range(8):
            hit = columns[0:SLOT, o : o + 1] == row
            left[width + o * SLOT : width + (o + 1) * SLOT, m * group : (m + 1) * group] = jnp.where(hit, 1.0, 0.0).astype(jnp.bfloat16)
    loads[1].wait()
    bucket[...] = dot(left[width:, 0:group], resid[0]) + dot(left[width:, group : 2 * group], resid[1])
    loads[0].wait()
    for m in range(micro):
        for k in range(2):
            first = rows * (1 - core) if k == 0 else rows * core
            block = emb[m, :, k * rows : (k + 1) * rows].T
            left[pl.ds(pl.multiple_of(first, rows), rows), m * group : (m + 1) * group] = block
    loads[2].wait()

    def sent(copy):
        copy.wait_send()

    def drain(c):
        each_own(c, sent)
        for far in (1, 2, 3):
            each_forward(c, far, sent, False)
        each_relay(c, sent, False)
        part_copy(c).wait_send()
        q_copy(c).wait_send()
        s_copy(c).wait_send()
        final_copy(c).wait()
        out_copy(c).wait()

    def slot(s, carry):
        guarded(s + LEAD - 1, lambda c: each_own(c, start))
        guarded(s - 1, forward_stage(1))
        guarded(s - 2, forward_stage(2))
        guarded(s - 3, forward_stage(3))
        guarded(s - 4, compute)
        guarded(s - 5, core_sum)
        guarded(s - 7, finish)
        guarded(s - 8, drain)
        return carry

    lax.fori_loop(1, CHUNKS + 3, slot, 0)

    def drain_some(low, high):
        def one(c, carry):
            drain(c)
            return carry

        lax.fori_loop(max(low, 0), high, one, 0)

    half = b_send.shape[1]

    def half_cols(k):
        return pl.ds(pl.multiple_of(k * half, half), half)

    b_copy = sibling_copy(b_send, b_recv, b_sem)
    compute(CHUNKS - 1)
    b_send[...] = bucket[:, half_cols(1 - core)]
    b_copy.start()
    core_sum(CHUNKS - 2)
    b_copy.wait_recv()
    y_send[...] = bucket[:, half_cols(core)] + b_recv[...]
    rows_copy = y_copy(y_send, y_recv, y_sem)
    rows_copy.start()
    core_sum(CHUNKS - 1)
    finish(CHUNKS - 4)
    drain_some(CHUNKS - 5, CHUNKS - 4)
    finish(CHUNKS - 3)
    rows_copy.wait_recv()
    a_send[...] = y_send[...] + y_recv[...]

    def a_copy(step):
        to = (me + step) % 8
        return pltpu.make_async_remote_copy(
            src_ref=a_send.at[pl.ds(pl.multiple_of(to * SLOT, SLOT), SLOT), :],
            dst_ref=a_recv.at[me],
            send_sem=a_send_sem.at[step],
            recv_sem=a_recv_sem.at[me],
            device_id=(dp, to),
            device_id_type=MESH,
        )

    def a_arrived(step):
        origin = (me + 8 - step) % 8
        return pltpu.make_async_remote_copy(
            src_ref=a_send.at[pl.ds(0, SLOT), :],
            dst_ref=a_recv.at[origin],
            send_sem=a_send_sem.at[step],
            recv_sem=a_recv_sem.at[origin],
            device_id=(dp, origin),
            device_id_type=MESH,
        )

    for step in range(1, 8):
        a_copy(step).start()
    a_recv[me] = a_send[pl.ds(pl.multiple_of(me * SLOT, SLOT), SLOT), :]
    finish(CHUNKS - 2)
    drain_some(CHUNKS - 4, CHUNKS - 3)
    for step in range(1, 8):
        a_arrived(step).wait_recv()
    h_copy = sibling_copy(a_recv, sib_recv, h_sem)
    h_copy.start()
    finish(CHUNKS - 1)
    drain_some(CHUNKS - 3, CHUNKS - 1)
    h_copy.wait_recv()
    for t in range(8):
        for k in range(2):
            at = (t % 2) * 2 * half + k * half
            piece = jnp.where(core == k, a_recv[t], sib_recv[t])
            grads_out[:, t // 2, at : at + half] = piece[0:entries]

    h_copy.wait_send()
    b_copy.wait_send()
    rows_copy.wait_send()
    for step in range(1, 8):
        a_copy(step).wait_send()

    drain_some(CHUNKS - 1, CHUNKS)


def fused(
    embedded,
    resid_grad,
    query_grad,
    query_weight,
    ngram_rows,
    touched_rows,
    row_values,
    row_mean,
    row_square,
):
    micro, group, width = embedded.shape
    hidden = query_grad.shape[2]
    tables = touched_rows.shape[0]
    entries = touched_rows.shape[2]
    cols, half, rows = hidden // CHUNKS, width // 2, width // 2
    slots = tables * SLOT
    f32, bf16, i16 = jnp.float32, jnp.bfloat16, jnp.int16
    dma = pltpu.SemaphoreType.DMA
    vmem = pltpu.VMEM
    anywhere = pl.BlockSpec(memory_space=pl.ANY)
    in_hbm = pl.BlockSpec(memory_space=pltpu.HBM)
    in_vmem = pl.BlockSpec(memory_space=pltpu.VMEM)
    operands = (embedded, resid_grad, query_grad, query_weight, ngram_rows.transpose(0, 2, 1), touched_rows)
    operands = [pltpu.with_memory_space_constraint(operand, pltpu.HBM) for operand in operands]
    weight_grad, grads, lists = pl.pallas_call(
        kernel,
        out_shape=(
            jax.ShapeDtypeStruct((width, hidden), f32),
            jax.ShapeDtypeStruct((entries, SLICES, SW), f32),
            jax.ShapeDtypeStruct((entries, SLICES, SW), f32),
        ),
        in_specs=[in_hbm] * 6,
        out_specs=(anywhere, in_vmem, in_vmem),
        scratch_shapes=[
            vmem((micro, SLICES, group), jnp.int32),
            vmem(touched_rows.shape, jnp.int32),
            vmem((128, 128), f32),
            vmem((micro, group, width), bf16),
            vmem((width + slots, micro * group), bf16),
            vmem((micro, group, width), bf16),
            vmem((width, hidden), bf16),
            vmem((CHUNKS, micro, group, cols), bf16),
            vmem((CHUNKS, width + slots, cols), f32),
            vmem((CHUNKS, rows, cols), f32),
            vmem((CHUNKS, rows, cols), i16),
            vmem((CHUNKS, rows, cols), i16),
            vmem((CHUNKS, 8, cols), f32),
            vmem((CHUNKS, 8, cols), f32),
            vmem((CHUNKS, rows, cols), f32),
            vmem((slots, width), f32),
            vmem((slots, half), f32),
            vmem((slots, half), f32),
            vmem((slots, half), f32),
            vmem((slots, half), f32),
            vmem((slots, half), f32),
            vmem((tables, SLOT, half), f32),
            vmem((tables, SLOT, half), f32),
            dma((5 + CHUNKS,)),
            dma((CHUNKS, tables, 3)),
            dma((CHUNKS, tables)),
            dma((CHUNKS, 2)),
            dma((CHUNKS, 2)),
            dma((CHUNKS, 2)),
            dma((CHUNKS, 2)),
            dma((CHUNKS,)),
            dma((2,)),
            dma((2,)),
            dma((tables,)),
            dma((tables,)),
            dma((2,)),
        ],
        compiler_params=pltpu.CompilerParams(
            collective_id=0, has_side_effects=True, vmem_limit_bytes=40 * 1024 * 1024
        ),
        cost_estimate=pl.CostEstimate(flops=3 * 10**9, bytes_accessed=2 * 10**7, transcendentals=0),
    )(*operands)

    def turned(rows):
        return rows[0].transpose(1, 0, 2)

    after = adam_rows(grads, turned(row_values), turned(row_mean), turned(row_square), lists >= 0)
    values_next, mean_next, square_next = [rows.transpose(1, 0, 2)[None] for rows in after]
    return (weight_grad, values_next, mean_next, square_next)


def solution(mesh):
    placed = (
        P(None, "dp", "table"),
        P(None, "dp", "table"),
        P(None, ("dp", "table"), None),
        P("table", None),
        P(None, "dp", None),
        P(),
        P("table", None, None, None),
        P("table", None, None, None),
        P("table", None, None, None),
    )
    fits = mesh.shape["dp"] == 4 and mesh.shape["table"] == 8
    return jax.shard_map(
        fused if fits else local,
        mesh=mesh,
        in_specs=placed,
        out_specs=(
            P("table", None),
            P("table", None, None, None),
            P("table", None, None, None),
            P("table", None, None, None),
        ),
        check_vma=False,
    )
```
